256 devices in a mesh: tm: 32 (over z, y), freq: 8 (over x, core).
Axes of the slice: x: 4, y: 4, z: 8, core: 2. Of those that a mesh axis runs over, the one named last changes fastest.
Arguments:
- snapshots: bfloat16 [4096, 32768], P('tm', 'freq'), may hold values from -8 to 8
Outputs:
- basis: bfloat16 [120, 62, 32768], P('freq', None, 'tm')
- factor: float32 [120, 62, 62], P('freq')
The draws below stay inside these ranges and needn't reach their ends.
All inputs are finite; a program needn't handle non-finite values.
Results may differ from the reference program's by a relative error of at most 0.0065.
Values may be sent and summed in bfloat16 or wider, within the bound.
A program may use at most 128 MiB of HBM per device.

```python
import math
import jax
import jax.numpy as jnp
from jax import lax

HOP = 128
K = 120
ROWS = 32768
NT = 4096
BLOCKS = 31
COLS = 62
N_TM = 32
N_FREQ = 8


def draw_snapshots(key, part):
    key = jax.random.fold_in(key, 11)
    key_rows, key_shard, key_noise = jax.random.split(key, 3)
    row_pos = jnp.arange(ROWS, dtype=jnp.float32) / ROWS
    row_scale = jnp.exp(math.log(3.0) * row_pos) * jnp.exp(jax.random.uniform(key_rows, (ROWS,), jnp.float32) * math.log(4.0))
    shard_scale = jnp.exp(jax.random.uniform(key_shard, (N_TM,), jnp.float32) * math.log(4.0))
    time_pos = jnp.arange(NT, dtype=jnp.int32)
    time_scale = jnp.exp(math.log(3.0) * time_pos.astype(jnp.float32) / NT) * jnp.repeat(shard_scale, HOP)
    noise = jnp.clip(jax.random.normal(key_noise, (NT, ROWS), jnp.float32), -5.0, 5.0)
    values = 0.01 * time_scale[:, None] * row_scale[None, :] * noise
    return values.astype(jnp.bfloat16)


def setup_inputs(seed: int = 0) -> dict:
    arg_keys = jax.random.split(jax.random.key(seed), 2)
    return {
        "snapshots": draw_snapshots(jax.random.fold_in(arg_keys[1], 71), 0),
    }


def fourier_table(num_bins, half_len, which_half):
    bins_col = jnp.arange(1, num_bins + 1, dtype=jnp.int32)[:, None]
    sample = jnp.arange(half_len, dtype=jnp.int32)[None, :] + which_half * half_len
    length = 2 * half_len
    phase_idx = (bins_col * sample % length).astype(jnp.float32) * (2.0 * math.pi / length)
    window = 0.5 - 0.5 * jnp.cos(sample.astype(jnp.float32) * (2.0 * math.pi / length))
    stacked = jnp.stack([window * jnp.cos(phase_idx), -window * jnp.sin(phase_idx)], axis=1)
    return stacked.reshape(2 * num_bins, half_len).astype(jnp.bfloat16)

def orthogonalize(columns):
    high = lax.Precision.HIGHEST
    as_float = columns.astype(jnp.float32)
    gram_matrix = jnp.einsum('fcr,fdr->fcd', as_float, as_float, precision=high) / ROWS
    lower_factor = jnp.linalg.cholesky(gram_matrix)
    identity = jnp.broadcast_to(jnp.eye(COLS, dtype=jnp.float32), gram_matrix.shape)
    inverse_lower = jax.scipy.linalg.solve_triangular(lower_factor, identity, lower=True)
    basis_full = jnp.einsum('fcd,fdr->fcr', inverse_lower, as_float, precision=high)
    return (basis_full.astype(jnp.bfloat16), jnp.transpose(lower_factor, (0, 2, 1)))

def reference(snapshots):
    halves = snapshots.reshape(N_TM, HOP, ROWS)
    per_group = K // N_FREQ
    own_tables = fourier_table(K, HOP, 0).reshape(N_FREQ, 2 * per_group, HOP)
    next_tables = fourier_table(K, HOP, 1).reshape(N_FREQ, 2 * per_group, HOP)

    def one_group(tables):
        own_table = tables[0].astype(jnp.float32)
        next_table = tables[1].astype(jnp.float32)

        def one_half(samples):
            as_float = samples.astype(jnp.float32)
            return (jnp.dot(own_table, as_float, precision=lax.Precision.HIGHEST), jnp.dot(next_table, as_float, precision=lax.Precision.HIGHEST))
        own_terms, next_terms = lax.map(one_half, halves)
        rounded = lax.optimization_barrier(next_terms[1:].astype(jnp.bfloat16))
        spectra = (own_terms[:BLOCKS] + rounded.astype(jnp.float32)).astype(jnp.bfloat16)
        spectra = spectra.reshape(BLOCKS, per_group, 2, ROWS).transpose(1, 2, 0, 3)
        return orthogonalize(spectra.reshape(per_group, COLS, ROWS))
    basis, factor = lax.map(one_group, (own_tables, next_tables))
    return (basis.reshape(K, COLS, ROWS), factor.reshape(K, COLS, COLS))
```

```python
import math

import jax
import jax.numpy as jnp
import numpy as np
from jax import lax
from jax.experimental import pallas as pl
from jax.experimental.pallas import tpu as pltpu
from jax.sharding import PartitionSpec as P

MESH = pl.DeviceIdType.MESH
K = 120
HALF = 128
TM = 32
FREQ = 8
BINS = K // FREQ
BLOCKS = TM - 1
COLS = 2 * BLOCKS
GROUP = 8
GROUPS = TM // GROUP
TILE = 2 * GROUP
PART = BINS * TILE
LANES = 128
SLABS = GROUP + 1
DEPTH = SLABS * HALF
SUB = 4
ROWS_HERE = FREQ * LANES
TOTAL_ROWS = TM * ROWS_HERE


def band_table():
    bins = np.arange(1, K + 1, dtype=np.int64)[:, None]
    sample = np.arange(2 * HALF, dtype=np.int64)[None, :]
    phase = (bins * sample % (2 * HALF)) * (2.0 * math.pi / (2 * HALF))
    window = 0.5 - 0.5 * np.cos(sample * (2.0 * math.pi / (2 * HALF)))
    table = np.stack([window * np.cos(phase), -window * np.sin(phase)], axis=1)
    table = table.astype(np.float32)
    band = np.zeros((K, 2, GROUP, SLABS * HALF), np.float32)
    for b in range(GROUP):
        band[:, :, b, b * HALF : (b + 2) * HALF] = table
    return band.reshape(K * TILE, DEPTH).astype(jnp.bfloat16)


def nt_dot(a, b):
    return lax.dot_general(a, b, (((1,), (1,)), ((), ())), preferred_element_type=jnp.float32)


def natural_rows(dst, value):
    for p in range(2):
        for g in range(GROUPS):
            r = TILE * g + GROUP * p
            dst[pl.ds(BLOCKS * p + GROUP * g, GROUP), :] = value[r : r + GROUP, :]


def eliminate(m):
    row = lax.broadcasted_iota(jnp.int32, (8, 128), 0)
    full = (8, 128)
    for j in range(0, COLS, 2):
        b, s = divmod(j, 8)
        r0 = jnp.broadcast_to(m[b][s : s + 1, :], full)
        r1 = jnp.broadcast_to(m[b][s + 1 : s + 2, :], full)
        a00 = jnp.broadcast_to(m[b][s : s + 1, j : j + 1], full)
        a01 = jnp.broadcast_to(m[b][s : s + 1, j + 1 : j + 2], full)
        a11 = jnp.broadcast_to(m[b][s + 1 : s + 2, j + 1 : j + 2], full)
        i0 = lax.rsqrt(a00)
        l10 = a01 * i0
        i1 = lax.rsqrt(a11 - l10 * l10)
        q0 = r0 * i0
        q1 = (r1 - l10 * q0) * i1
        for i in range(b, 8):
            c0 = jnp.broadcast_to(m[i][:, j : j + 1], full)
            c1 = jnp.broadcast_to(m[i][:, j + 1 : j + 2], full)
            m0 = c0 * i0
            m1 = (c1 - l10 * m0) * i1
            u = m[i] - m0 * q0 - m1 * q1
            if i == b:
                u = jnp.where(row > s + 1, u, m[i])
                u = jnp.where(row == s, q0, u)
                u = jnp.where(row == s + 1, q1, u)
            m[i] = u
    return m


def kernel(
    x_ref, band_hbm, basis_ref, factor_ref,
    band, mid, xt, spec, held, cols, gpart, grecv, res, perm,
    band_sem, l_sem, a_send, a_recv, b_send, b_recv, c_send, c_recv,
    g_send, g_recv, r_send, r_recv,
):
    t = lax.axis_index("tm")
    f = lax.axis_index("freq")
    z, y = t // SUB, t % SUB

    def colblock(j):
        return x_ref.at[:, pl.ds(pl.multiple_of(j * LANES, LANES), LANES)]

    def freq_peer(i):
        return lax.rem(f + i, FREQ)

    def tm_peer(i):
        return lax.rem(t + i, TM)

    def remote(src, dst, send, recv, to):
        return pltpu.make_async_remote_copy(
            src, dst, send, recv, device_id=to, device_id_type=MESH
        )

    def each(lo, hi, body):
        def step(i, carry):
            body(i)
            return carry

        lax.fori_loop(lo, hi, step, 0)

    load_band = pltpu.make_async_copy(band_hbm, band, band_sem)
    load_band.start()

    barrier = pltpu.get_barrier_semaphore()
    each(1, FREQ, lambda i: pl.semaphore_signal(
        barrier, inc=1, device_id=(t, freq_peer(i)), device_id_type=MESH))
    each(1, TM, lambda i: pl.semaphore_signal(
        barrier, inc=1, device_id=(tm_peer(i), f), device_id_type=MESH))
    pl.semaphore_wait(barrier, FREQ - 1 + TM - 1)

    def a_copy(i, s):
        to = freq_peer(i)
        return remote(colblock(FREQ * s + to), mid.at[SUB * f + s], a_send.at[i, s],
                      a_recv.at[f, s], (t, to))

    for s in range(SUB):
        each(1, FREQ, lambda i: a_copy(i, s).start())
        pltpu.make_async_copy(colblock(FREQ * s + f), mid.at[SUB * f + s], l_sem.at[s]).start()
    for s in range(SUB):
        pltpu.make_async_copy(colblock(FREQ * s + f), mid.at[SUB * f + s], l_sem.at[s]).wait()

    xt[TM] = jnp.zeros((HALF, LANES), jnp.bfloat16)

    def b_copy(n):
        return remote(mid.at[n], xt.at[t], b_send.at[n], b_recv.at[t], (n, f))

    def b_step(i):
        d = i // SUB
        dz = jnp.where(d % 2 == 1, (d + 1) // 2, FREQ - d // 2)
        ff = lax.rem(z + dz, FREQ)
        s = lax.rem(y + i, SUB)
        n = SUB * ff + s

        @pl.when(ff != f)
        def _():
            remote(mid.at[n], mid.at[n], a_send.at[0, 0], a_recv.at[ff, s], (t, f)).wait_recv()

        @pl.when(n != t)
        def _():
            b_copy(n).start()

        @pl.when(n == t)
        def _():
            pltpu.make_async_copy(mid.at[n], xt.at[t], l_sem.at[0]).start()

    each(0, TM, b_step)
    pltpu.make_async_copy(mid.at[t], xt.at[t], l_sem.at[0]).wait()
    load_band.wait()

    first = lax.rem(lax.rem(z + FREQ - 1, FREQ) // 2, GROUPS)

    def lanes_of(ff):
        return pl.ds(pl.multiple_of(ff * LANES, LANES), LANES)

    def piece(ff):
        return pl.ds(pl.multiple_of(ff * PART, PART), PART)

    def c_copy(i, g):
        to = freq_peer(i)
        return remote(spec.at[g, piece(to), :], held.at[g, :, lanes_of(f)],
                      c_send.at[i, g], c_recv.at[f, g], (t, to))

    def wait_slab(i):
        n = lax.rem(GROUP * first + i, TM)

        @pl.when(n != t)
        def _():
            remote(xt.at[n], xt.at[n], b_send.at[0], b_recv.at[n], (t, f)).wait_recv()

    def make_group(step, carry):
        g = lax.rem(first + step, GROUPS)
        lo = jnp.where(step == 0, 0, GROUP * step + 1)
        hi = jnp.minimum(GROUP * step + GROUP + 1, TM)
        each(lo, hi, wait_slab)
        stack = xt[pl.ds(GROUP * g, SLABS)].reshape(DEPTH, LANES)

        def part(i):
            to = freq_peer(i)
            rows = piece(to)
            value = jnp.dot(band[rows, :], stack, preferred_element_type=jnp.float32)
            spec[g, rows, :] = value.astype(jnp.bfloat16)

        def send_part(i):
            part(i)
            c_copy(i, g).start()

        each(1, FREQ, send_part)
        part(0)
        pltpu.make_async_copy(spec.at[g, piece(f), :], held.at[g, :, lanes_of(f)], l_sem.at[g]).start()
        return carry

    lax.fori_loop(0, GROUPS, make_group, 0)

    def wait_group(g):
        pltpu.make_async_copy(spec.at[g, piece(f), :], held.at[g, :, lanes_of(f)], l_sem.at[g]).wait()

        def wait_piece(i):
            ff = freq_peer(i)
            remote(spec.at[g, piece(ff), :], held.at[g, :, lanes_of(ff)],
                   c_send.at[0, 0], c_recv.at[ff, g], (t, f)).wait_recv()

        each(1, FREQ, wait_piece)

    each(0, GROUPS, wait_group)

    def owner(k):
        return 2 * k + f % 2

    def bin_columns(k):
        return jnp.concatenate(
            [held[g, pl.ds(pl.multiple_of(TILE * k, TILE), TILE), :] for g in range(GROUPS)], axis=0)

    def g_copy(k):
        return remote(gpart.at[k], grecv.at[t], g_send.at[k], g_recv.at[t], (owner(k), f))

    def gram(k):
        a = bin_columns(k)
        gm = nt_dot(a, a)
        gpart[k] = jnp.concatenate([gm[:32], gm[32:]], axis=1)

        @pl.when(owner(k) != t)
        def _():
            g_copy(k).start()

        @pl.when(owner(k) == t)
        def _():
            pltpu.make_async_copy(gpart.at[k], grecv.at[t], l_sem.at[0]).start()

    each(0, BINS, gram)

    r = lax.broadcasted_iota(jnp.int32, (64, 64), 0)
    c = lax.broadcasted_iota(jnp.int32, (64, 64), 1)
    block = GROUP * (c // TILE) + c % GROUP
    to_row = BLOCKS * (c % TILE // GROUP) + block
    order = jnp.where((r == to_row) & (block < BLOCKS), 1.0, 0.0).astype(jnp.bfloat16)

    def reorder(k):
        cols[k] = jnp.dot(order, bin_columns(k), preferred_element_type=jnp.float32).astype(
            jnp.bfloat16)

    each(0, BINS, reorder)

    mine = t // 2
    is_owner = (t % 2 == f % 2) & (mine < BINS)

    def r_copy(i):
        return remote(res.at[mine], res.at[mine], r_send.at[i], r_recv.at[mine], (tm_peer(i), f))

    @pl.when(is_owner)
    def _():
        pltpu.make_async_copy(gpart.at[mine], grecv.at[t], l_sem.at[0]).wait()

        def g_wait(i):
            n = tm_peer(i)
            remote(grecv.at[n], grecv.at[n], g_send.at[0], g_recv.at[n], (t, f)).wait_recv()

        each(1, TM, g_wait)
        total = grecv[0]
        for n in range(1, TM):
            total = total + grecv[n]
        total = total * (1.0 / TOTAL_ROWS)
        gm = jnp.concatenate([total[:, :64], total[:, 64:]], axis=0)
        perm[...] = jnp.zeros_like(perm)
        natural_rows(perm, gm)
        gm = perm[0:64, :].T
        natural_rows(perm, gm)
        eye = jnp.where(r == c, 1.0, 0.0).astype(jnp.float32)
        m = jnp.concatenate([perm[0:64, :], eye], axis=1)
        m = eliminate([m[8 * i : 8 * i + 8, :] for i in range(8)])
        for i in range(8):
            res[mine, 8 * i : 8 * i + 8, :] = m[i]
        each(1, TM, lambda i: r_copy(i).start())

    upper = c >= r

    def finish(k):
        @pl.when(jnp.logical_not(is_owner & (mine == k)))
        def _():
            remote(res.at[k], res.at[k], r_send.at[0], r_recv.at[k], (t, f)).wait_recv()

        v = res[k]
        factor_ref[k] = jnp.where(upper, v[:, :64], 0.0)[:COLS, :COLS]
        w = jnp.where(c <= r, v[:, 64:], 0.0)
        hi = w.astype(jnp.bfloat16)
        rest = w - hi.astype(jnp.float32)
        lo = rest.astype(jnp.bfloat16)
        low = (rest - lo.astype(jnp.float32)).astype(jnp.bfloat16)
        a = cols[k]
        out = jnp.dot(low, a, preferred_element_type=jnp.float32)
        out = out + jnp.dot(lo, a, preferred_element_type=jnp.float32)
        out = out + jnp.dot(hi, a, preferred_element_type=jnp.float32)
        basis_ref[k] = out[:COLS, :].astype(jnp.bfloat16)

    each(0, BINS, finish)

    for s in range(SUB):
        each(1, FREQ, lambda i: a_copy(i, s).wait_send())

    def b_wait(n):
        @pl.when(n != t)
        def _():
            b_copy(n).wait_send()

    each(0, TM, b_wait)
    for g in range(GROUPS):
        each(1, FREQ, lambda i: c_copy(i, g).wait_send())

    def g_wait_send(k):
        @pl.when(owner(k) != t)
        def _():
            g_copy(k).wait_send()

    each(0, BINS, g_wait_send)

    @pl.when(is_owner)
    def _():
        each(1, TM, lambda i: r_copy(i).wait_send())


def on_device(snapshots):
    band = jnp.asarray(band_table())
    bf16, f32 = jnp.bfloat16, jnp.float32
    dma = pltpu.SemaphoreType.DMA
    anywhere = pl.BlockSpec(memory_space=pl.ANY)
    vmem = pl.BlockSpec(memory_space=pltpu.VMEM)
    return pl.pallas_call(
        kernel,
        out_shape=(
            jax.ShapeDtypeStruct((BINS, COLS, ROWS_HERE), bf16),
            jax.ShapeDtypeStruct((BINS, COLS, COLS), f32),
        ),
        in_specs=[anywhere, anywhere],
        out_specs=(vmem, vmem),
        scratch_shapes=[
            pltpu.VMEM((K * TILE, DEPTH), bf16),
            pltpu.VMEM((TM, HALF, LANES), bf16),
            pltpu.VMEM((TM + 1, HALF, LANES), bf16),
            pltpu.VMEM((GROUPS, K * TILE, LANES), bf16),
            pltpu.VMEM((GROUPS, PART, ROWS_HERE), bf16),
            pltpu.VMEM((BINS, 64, ROWS_HERE), bf16),
            pltpu.VMEM((BINS, 32, 128), f32),
            pltpu.VMEM((TM, 32, 128), f32),
            pltpu.VMEM((BINS, 64, 128), f32),
            pltpu.VMEM((72, 64), f32),
            dma,
            dma((GROUPS,)),
            dma((FREQ, SUB)),
            dma((FREQ, SUB)),
            dma((TM,)),
            dma((TM,)),
            dma((FREQ, GROUPS)),
            dma((FREQ, GROUPS)),
            dma((BINS,)),
            dma((TM,)),
            dma((TM,)),
            dma((BINS,)),
        ],
        name="block_spectra_qr",
        compiler_params=pltpu.CompilerParams(
            collective_id=0, has_side_effects=True, vmem_limit_bytes=40 * 2**20
        ),
    )(snapshots, band)


def solution(mesh):
    return jax.shard_map(
        on_device,
        mesh=mesh,
        in_specs=(P("tm", "freq"),),
        out_specs=(P("freq", None, "tm"), P("freq", None, None)),
        check_vma=False,
    )
```

```python
import math

import jax
import jax.numpy as jnp
import numpy as np
from jax import lax
from jax.experimental import pallas as pl
from jax.experimental.pallas import tpu as pltpu
from jax.sharding import PartitionSpec as P

MESH = pl.DeviceIdType.MESH
K = 120
HALF = 128
TM = 32
FREQ = 8
BINS = K // FREQ
BLOCKS = TM - 1
COLS = 2 * BLOCKS
GROUP = 8
GROUPS = TM // GROUP
TILE = 2 * GROUP
PART = BINS * TILE
LANES = 128
SLABS = GROUP + 1
DEPTH = SLABS * HALF
SUB = 4
ROWS_HERE = FREQ * LANES
B_ORDER = (2, 6, 0, 4, 1, 7, 3, 5)
B_EARLY = 3
B_FLIGHT = 8
TOTAL_ROWS = TM * ROWS_HERE


def band_table():
    bins = np.arange(1, K + 1, dtype=np.int64)[:, None]
    sample = np.arange(2 * HALF, dtype=np.int64)[None, :]
    phase = (bins * sample % (2 * HALF)) * (2.0 * math.pi / (2 * HALF))
    window = 0.5 - 0.5 * np.cos(sample * (2.0 * math.pi / (2 * HALF)))
    table = np.stack([window * np.cos(phase), -window * np.sin(phase)], axis=1)
    table = table.astype(np.float32)
    band = np.zeros((K, 2, GROUP, SLABS * HALF), np.float32)
    for b in range(GROUP):
        band[:, :, b, b * HALF : (b + 2) * HALF] = table
    return band.reshape(K * TILE, DEPTH).astype(jnp.bfloat16)


def nt_dot(a, b):
    return lax.dot_general(a, b, (((1,), (1,)), ((), ())), preferred_element_type=jnp.float32)


def natural_rows(dst, value):
    for p in range(2):
        for g in range(GROUPS):
            r = TILE * g + GROUP * p
            dst[pl.ds(BLOCKS * p + GROUP * g, GROUP), :] = value[r : r + GROUP, :]


def eliminate(m):
    row = lax.broadcasted_iota(jnp.int32, (8, 128), 0)
    full = (8, 128)
    for j in range(0, COLS, 2):
        b, s = divmod(j, 8)
        r0 = jnp.broadcast_to(m[b][s : s + 1, :], full)
        r1 = jnp.broadcast_to(m[b][s + 1 : s + 2, :], full)
        a00 = jnp.broadcast_to(m[b][s : s + 1, j : j + 1], full)
        a01 = jnp.broadcast_to(m[b][s : s + 1, j + 1 : j + 2], full)
        a11 = jnp.broadcast_to(m[b][s + 1 : s + 2, j + 1 : j + 2], full)
        i0 = lax.rsqrt(a00)
        l10 = a01 * i0
        i1 = lax.rsqrt(a11 - l10 * l10)
        q0 = r0 * i0
        q1 = (r1 - l10 * q0) * i1
        for i in range(b, 8):
            c0 = jnp.broadcast_to(m[i][:, j : j + 1], full)
            c1 = jnp.broadcast_to(m[i][:, j + 1 : j + 2], full)
            m0 = c0 * i0
            m1 = (c1 - l10 * m0) * i1
            u = m[i] - m0 * q0 - m1 * q1
            if i == b:
                u = jnp.where(row > s + 1, u, m[i])
                u = jnp.where(row == s, q0, u)
                u = jnp.where(row == s + 1, q1, u)
            m[i] = u
    return m


def kernel(
    x_ref, band_hbm, basis_ref, factor_ref,
    band, mid, xt, spec, held, cols, gpart, grecv, res, perm,
    band_sem, l_sem, a_send, a_recv, b_send, b_recv, c_send, c_recv,
    g_send, g_recv, z_send, y_send, r_recv,
):
    t = lax.axis_index("tm")
    f = lax.axis_index("freq")
    z, y = t // SUB, t % SUB

    def colblock(j):
        return x_ref.at[:, pl.ds(pl.multiple_of(j * LANES, LANES), LANES)]

    def freq_peer(i):
        return lax.rem(f + i, FREQ)

    def tm_peer(i):
        return lax.rem(t + i, TM)

    def remote(src, dst, send, recv, to):
        return pltpu.make_async_remote_copy(
            src, dst, send, recv, device_id=to, device_id_type=MESH
        )

    def each(lo, hi, body):
        def step(i, carry):
            body(i)
            return carry

        lax.fori_loop(lo, hi, step, 0)

    load_band = pltpu.make_async_copy(band_hbm, band, band_sem)
    load_band.start()

    barrier = pltpu.get_barrier_semaphore()
    each(1, FREQ, lambda i: pl.semaphore_signal(
        barrier, inc=1, device_id=(t, freq_peer(i)), device_id_type=MESH))
    each(1, TM, lambda i: pl.semaphore_signal(
        barrier, inc=1, device_id=(tm_peer(i), f), device_id_type=MESH))
    pl.semaphore_wait(barrier, FREQ - 1 + TM - 1)

    def a_copy(i, s):
        to = freq_peer(i)
        return remote(colblock(FREQ * s + to), mid.at[SUB * f + s], a_send.at[i, s],
                      a_recv.at[f, s], (t, to))

    def own_copy(s):
        return pltpu.make_async_copy(colblock(FREQ * s + f), mid.at[SUB * f + s], l_sem.at[s])

    away = lax.rem(f - z + FREQ, FREQ)
    early = away % 2 == 0

    def a_start():
        for s in range(SUB):
            each(1, FREQ, lambda i: a_copy(i, s).start())

    pl.when(early)(a_start)
    for s in range(SUB):
        own_copy(s).start()
    xt[TM] = jnp.zeros((HALF, LANES), jnp.bfloat16)
    for s in range(SUB):
        own_copy(s).wait()

    def b_copy(n):
        return remote(mid.at[n], xt.at[t], b_send.at[n], b_recv.at[t], (n, f))

    def b_steps(dz):
        ff = lax.rem(z + dz, FREQ)

        def b_step(i):
            s = lax.rem(y + i, SUB)
            n = SUB * ff + s

            @pl.when(ff != f)
            def _():
                remote(mid.at[n], mid.at[n], a_send.at[0, 0], a_recv.at[ff, s], (t, f)).wait_recv()

            @pl.when(n != t)
            def _():
                b_copy(n).start()

            @pl.when(n == t)
            def _():
                pltpu.make_async_copy(mid.at[n], xt.at[t], l_sem.at[0]).start()

        each(0, SUB, b_step)

    def b_done(dz):
        ff = lax.rem(z + dz, FREQ)

        def b_wait(i):
            n = SUB * ff + lax.rem(y + i, SUB)

            @pl.when(n != t)
            def _():
                b_copy(n).wait_send()

        each(0, SUB, b_wait)

    for i, dz in enumerate(B_ORDER):
        if i == B_EARLY:
            pl.when(jnp.logical_not(early))(a_start)
        if i >= B_FLIGHT:
            b_done(B_ORDER[i - B_FLIGHT])
        b_steps(dz)
    pltpu.make_async_copy(mid.at[t], xt.at[t], l_sem.at[0]).wait()
    load_band.wait()

    first = lax.rem(lax.rem(z + FREQ - 1, FREQ) // 2, GROUPS)

    def lanes_of(ff):
        return pl.ds(pl.multiple_of(ff * LANES, LANES), LANES)

    def piece(ff):
        return pl.ds(pl.multiple_of(ff * PART, PART), PART)

    def c_copy(i, g):
        to = freq_peer(i)
        return remote(spec.at[g, piece(to), :], held.at[g, :, lanes_of(f)],
                      c_send.at[i, g], c_recv.at[f, g], (t, to))

    def wait_slab(i):
        n = lax.rem(GROUP * first + i, TM)

        @pl.when(n != t)
        def _():
            remote(xt.at[n], xt.at[n], b_send.at[0], b_recv.at[n], (t, f)).wait_recv()

    def make_group(step, carry):
        g = lax.rem(first + step, GROUPS)
        lo = jnp.where(step == 0, 0, GROUP * step + 1)
        hi = jnp.minimum(GROUP * step + GROUP + 1, TM)
        each(lo, hi, wait_slab)
        stack = xt[pl.ds(GROUP * g, SLABS)].reshape(DEPTH, LANES)

        def part(i):
            to = freq_peer(i)
            rows = piece(to)
            value = jnp.dot(band[rows, :], stack, preferred_element_type=jnp.float32)
            spec[g, rows, :] = value.astype(jnp.bfloat16)

        def send_part(i):
            part(i)
            c_copy(i, g).start()

        for i in range(1, FREQ):
            send_part(i)
        part(0)
        pltpu.make_async_copy(spec.at[g, piece(f), :], held.at[g, :, lanes_of(f)], l_sem.at[g]).start()
        return carry

    lax.fori_loop(0, GROUPS, make_group, 0)

    def wait_group(g):
        pltpu.make_async_copy(spec.at[g, piece(f), :], held.at[g, :, lanes_of(f)], l_sem.at[g]).wait()

        def wait_piece(i):
            ff = freq_peer(i)
            remote(spec.at[g, piece(ff), :], held.at[g, :, lanes_of(ff)],
                   c_send.at[0, 0], c_recv.at[ff, g], (t, f)).wait_recv()

        each(1, FREQ, wait_piece)

    each(0, GROUPS, wait_group)

    def owner(k):
        return 2 * k + f % 2

    def bin_columns(k):
        return jnp.concatenate(
            [held[g, pl.ds(TILE * k, TILE), :] for g in range(GROUPS)], axis=0)

    def g_copy(k):
        return remote(gpart.at[k], grecv.at[t], g_send.at[k], g_recv.at[t], (owner(k), f))

    for k in range(BINS):
        a = bin_columns(k)
        gm = nt_dot(a, a)
        gpart[k] = jnp.concatenate([gm[:32], gm[32:]], axis=1)

    def g_start(k):
        @pl.when(owner(k) != t)
        def _():
            g_copy(k).start()

        @pl.when(owner(k) == t)
        def _():
            pltpu.make_async_copy(gpart.at[k], grecv.at[t], l_sem.at[0]).start()

    each(0, BINS, g_start)

    r = lax.broadcasted_iota(jnp.int32, (64, 64), 0)
    c = lax.broadcasted_iota(jnp.int32, (64, 64), 1)
    block = GROUP * (c // TILE) + c % GROUP
    to_row = BLOCKS * (c % TILE // GROUP) + block
    order = jnp.where((r == to_row) & (block < BLOCKS), 1.0, 0.0).astype(jnp.bfloat16)

    for k in range(BINS):
        cols[k] = jnp.dot(order, bin_columns(k), preferred_element_type=jnp.float32).astype(
            jnp.bfloat16)

    mine = t // 2
    in_column = t % 2 == f % 2
    is_owner = in_column & (mine < BINS)

    def z_copy(i):
        to = SUB * lax.rem(z + i, FREQ) + y
        return remote(res.at[mine], res.at[mine], z_send.at[i], r_recv.at[mine], (to, f))

    def y_copy(k, i):
        to = SUB * z + lax.rem(y + i, SUB)
        return remote(res.at[k], res.at[k], y_send.at[k // 2, i], r_recv.at[k], (to, f))

    def received(k):
        remote(res.at[k], res.at[k], z_send.at[0], r_recv.at[k], (t, f)).wait_recv()

    @pl.when(is_owner)
    def _():
        pltpu.make_async_copy(gpart.at[mine], grecv.at[t], l_sem.at[0]).wait()

        def g_wait(i):
            n = tm_peer(i)
            remote(grecv.at[n], grecv.at[n], g_send.at[0], g_recv.at[n], (t, f)).wait_recv()

        each(1, TM, g_wait)
        total = grecv[0]
        for n in range(1, TM):
            total = total + grecv[n]
        total = total * (1.0 / TOTAL_ROWS)
        gm = jnp.concatenate([total[:, :64], total[:, 64:]], axis=0)
        perm[...] = jnp.zeros_like(perm)
        natural_rows(perm, gm)
        gm = perm[0:64, :].T
        natural_rows(perm, gm)
        eye = jnp.where(r == c, 1.0, 0.0).astype(jnp.float32)
        m = jnp.concatenate([perm[0:64, :], eye], axis=1)
        m = eliminate([m[8 * i : 8 * i + 8, :] for i in range(8)])
        m = jnp.concatenate(m, axis=0)
        both = jnp.where(c >= r, m[:, :64], m[:, 64:])
        res[mine] = jnp.concatenate([both[:32], both[32:]], axis=1)
        each(1, FREQ, lambda i: z_copy(i).start())

    def relay(i):
        k = (SUB * lax.rem(z + i, FREQ) + y) // 2

        @pl.when(k < BINS)
        def _():
            @pl.when(i > 0)
            def _():
                received(k)

            each(1, SUB, lambda j: y_copy(k, j).start())

    @pl.when(in_column)
    def _():
        each(0, FREQ, relay)

    def arrived(k):
        @pl.when(jnp.logical_not(in_column & ((2 * k + f % 2) % SUB == y)))
        def _():
            received(k)

    each(0, BINS, arrived)
    for k in range(BINS):
        v = res[k]
        both = jnp.concatenate([v[:, :64], v[:, 64:]], axis=0)
        factor_ref[k] = jnp.where(c >= r, both, 0.0)[:COLS, :COLS]
        w = jnp.where(c < r, both, jnp.where(c == r, 1.0 / both, 0.0))
        hi = w.astype(jnp.bfloat16)
        rest = w - hi.astype(jnp.float32)
        lo = rest.astype(jnp.bfloat16)
        low = (rest - lo.astype(jnp.float32)).astype(jnp.bfloat16)
        a = cols[k]
        out = jnp.dot(low, a, preferred_element_type=jnp.float32)
        out = out + jnp.dot(lo, a, preferred_element_type=jnp.float32)
        out = out + jnp.dot(hi, a, preferred_element_type=jnp.float32)
        basis_ref[k] = out[:COLS, :].astype(jnp.bfloat16)

    for s in range(SUB):
        each(1, FREQ, lambda i: a_copy(i, s).wait_send())

    for dz in B_ORDER[FREQ - B_FLIGHT :]:
        b_done(dz)
    for g in range(GROUPS):
        each(1, FREQ, lambda i: c_copy(i, g).wait_send())

    def g_wait_send(k):
        @pl.when(owner(k) != t)
        def _():
            g_copy(k).wait_send()

    each(0, BINS, g_wait_send)

    @pl.when(is_owner)
    def _():
        each(1, FREQ, lambda i: z_copy(i).wait_send())

    def relay_wait(i):
        k = (SUB * lax.rem(z + i, FREQ) + y) // 2

        @pl.when(k < BINS)
        def _():
            each(1, SUB, lambda j: y_copy(k, j).wait_send())

    @pl.when(in_column)
    def _():
        each(0, FREQ, relay_wait)


def on_device(snapshots):
    band = jnp.asarray(band_table())
    bf16, f32 = jnp.bfloat16, jnp.float32
    dma = pltpu.SemaphoreType.DMA
    hbm = pl.BlockSpec(memory_space=pltpu.HBM)
    vmem = pl.BlockSpec(memory_space=pltpu.VMEM)
    return pl.pallas_call(
        kernel,
        out_shape=(
            jax.ShapeDtypeStruct((BINS, COLS, ROWS_HERE), bf16),
            jax.ShapeDtypeStruct((BINS, COLS, COLS), f32),
        ),
        in_specs=[hbm, hbm],
        out_specs=(vmem, vmem),
        scratch_shapes=[
            pltpu.VMEM((K * TILE, DEPTH), bf16),
            pltpu.VMEM((TM, HALF, LANES), bf16),
            pltpu.VMEM((TM + 1, HALF, LANES), bf16),
            pltpu.VMEM((GROUPS, K * TILE, LANES), bf16),
            pltpu.VMEM((GROUPS, PART, ROWS_HERE), bf16),
            pltpu.VMEM((BINS, 64, ROWS_HERE), bf16),
            pltpu.VMEM((BINS, 32, 128), f32),
            pltpu.VMEM((TM, 32, 128), f32),
            pltpu.VMEM((BINS, 32, 128), f32),
            pltpu.VMEM((72, 64), f32),
            dma,
            dma((GROUPS,)),
            dma((FREQ, SUB)),
            dma((FREQ, SUB)),
            dma((TM,)),
            dma((TM,)),
            dma((FREQ, GROUPS)),
            dma((FREQ, GROUPS)),
            dma((BINS,)),
            dma((TM,)),
            dma((FREQ,)),
            dma((FREQ, SUB)),
            dma((BINS,)),
        ],
        name="block_spectra_qr",
        compiler_params=pltpu.CompilerParams(
            collective_id=0, has_side_effects=True, vmem_limit_bytes=60 * 2**20
        ),
    )(snapshots, band)


def solution(mesh):
    return jax.shard_map(
        on_device,
        mesh=mesh,
        in_specs=(P("tm", "freq"),),
        out_specs=(P("freq", None, "tm"), P("freq", None, None)),
        check_vma=False,
    )
```

```python
import math

import jax
import jax.numpy as jnp
import numpy as np
from jax import lax
from jax.experimental import pallas as pl
from jax.experimental.pallas import tpu as pltpu
from jax.sharding import PartitionSpec as P

MESH = pl.DeviceIdType.MESH
K = 120
HALF = 128
TM = 32
FREQ = 8
BINS = K // FREQ
BLOCKS = TM - 1
COLS = 2 * BLOCKS
GROUP = 8
GROUPS = TM // GROUP
TILE = 2 * GROUP
PART = BINS * TILE
LANES = 128
SLABS = GROUP + 1
DEPTH = SLABS * HALF
SUB = 4
ROWS_HERE = FREQ * LANES
LAST_BINS = 3
CHUNKS = BINS // LAST_BINS
SPREAD = 11
H_BIN = (0, 11, BINS)
H_ROW = tuple(TILE * k for k in H_BIN[:2])
H_ROWS = tuple(TILE * (hi - lo) for lo, hi in zip(H_BIN, H_BIN[1:]))
B_ORDER = (2, 6, 4, 0, 1, 7, 3, 5)
B_EARLY = 4
TOTAL_ROWS = TM * ROWS_HERE


def band_table():
    bins = np.arange(1, K + 1, dtype=np.int64)[:, None]
    sample = np.arange(2 * HALF, dtype=np.int64)[None, :]
    phase = (bins * sample % (2 * HALF)) * (2.0 * math.pi / (2 * HALF))
    window = 0.5 - 0.5 * np.cos(sample * (2.0 * math.pi / (2 * HALF)))
    table = np.stack([window * np.cos(phase), -window * np.sin(phase)], axis=1)
    table = table.astype(np.float32)
    band = np.zeros((K, 2, GROUP, SLABS * HALF), np.float32)
    for b in range(GROUP):
        band[:, :, b, b * HALF : (b + 2) * HALF] = table
    return band.reshape(K * TILE, DEPTH).astype(jnp.bfloat16)


def nt_dot(a, b):
    return lax.dot_general(a, b, (((1,), (1,)), ((), ())), preferred_element_type=jnp.float32)


def natural_rows(dst, value):
    for p in range(2):
        for g in range(GROUPS):
            r = TILE * g + GROUP * p
            dst[pl.ds(BLOCKS * p + GROUP * g, GROUP), :] = value[r : r + GROUP, :]


def eliminate(m):
    row = lax.broadcasted_iota(jnp.int32, (8, 128), 0)
    full = (8, 128)
    for j in range(0, COLS, 2):
        b, s = divmod(j, 8)
        r0 = jnp.broadcast_to(m[b][s : s + 1, :], full)
        r1 = jnp.broadcast_to(m[b][s + 1 : s + 2, :], full)
        a00 = jnp.broadcast_to(m[b][s : s + 1, j : j + 1], full)
        a01 = jnp.broadcast_to(m[b][s : s + 1, j + 1 : j + 2], full)
        a11 = jnp.broadcast_to(m[b][s + 1 : s + 2, j + 1 : j + 2], full)
        i0 = lax.rsqrt(a00)
        l10 = a01 * i0
        i1 = lax.rsqrt(a11 - l10 * l10)
        q0 = r0 * i0
        q1 = (r1 - l10 * q0) * i1
        for i in range(b, 8):
            c0 = jnp.broadcast_to(m[i][:, j : j + 1], full)
            c1 = jnp.broadcast_to(m[i][:, j + 1 : j + 2], full)
            m0 = c0 * i0
            m1 = (c1 - l10 * m0) * i1
            u = m[i] - m0 * q0 - m1 * q1
            if i == b:
                u = jnp.where(row > s + 1, u, m[i])
                u = jnp.where(row == s, q0, u)
                u = jnp.where(row == s + 1, q1, u)
            m[i] = u
    return m


def kernel(
    x_ref, band_hbm, cols, res,
    band, mid, xt, spec, held, gpart, grecv, perm,
    band_sem, l_sem, a_send, a_recv, b_send, b_recv, c_send, c_recv,
    g_send, g_recv, z_send, z_recv, y_send, y_recv,
):
    t = lax.axis_index("tm")
    f = lax.axis_index("freq")
    z, y = t // SUB, t % SUB

    def colblock(j):
        return x_ref.at[:, pl.ds(pl.multiple_of(j * LANES, LANES), LANES)]

    def freq_peer(i):
        return lax.rem(f + i, FREQ)

    def tm_peer(i):
        return lax.rem(t + i, TM)

    def remote(src, dst, send, recv, to):
        return pltpu.make_async_remote_copy(
            src, dst, send, recv, device_id=to, device_id_type=MESH
        )

    def each(lo, hi, body):
        def step(i, carry):
            body(i)
            return carry

        lax.fori_loop(lo, hi, step, 0)

    load_band = pltpu.make_async_copy(band_hbm, band, band_sem)
    load_band.start()

    barrier = pltpu.get_barrier_semaphore()
    each(1, FREQ, lambda i: pl.semaphore_signal(
        barrier, inc=1, device_id=(t, freq_peer(i)), device_id_type=MESH))
    each(1, TM, lambda i: pl.semaphore_signal(
        barrier, inc=1, device_id=(tm_peer(i), f), device_id_type=MESH))
    pl.semaphore_wait(barrier, FREQ - 1 + TM - 1)

    def a_copy(i, s):
        to = freq_peer(i)
        return remote(colblock(FREQ * s + to), mid.at[SUB * f + s], a_send, a_recv.at[f], (t, to))

    def own_copy(s):
        return pltpu.make_async_copy(colblock(FREQ * s + f), mid.at[SUB * f + s], l_sem.at[s])

    away = lax.rem(f - z + FREQ, FREQ)
    early = away % 2 == 0

    def a_start():
        def a_peer(i):
            for s in range(SUB):
                a_copy(i, s).start()

        each(1, FREQ, a_peer)

    pl.when(early)(a_start)
    for s in range(SUB):
        own_copy(s).start()
    xt[TM] = jnp.zeros((HALF, LANES), jnp.bfloat16)
    for s in range(SUB):
        own_copy(s).wait()

    def b_copy(n):
        return remote(mid.at[n], xt.at[t], b_send, b_recv.at[t], (n, f))

    def b_steps(dz):
        ff = lax.rem(z + dz, FREQ)

        @pl.when(ff != f)
        def _():
            part = mid.at[pl.ds(SUB * ff, SUB)]
            remote(part, part, a_send, a_recv.at[ff], (t, f)).wait_recv()

        for i in range(SUB):
            n = SUB * ff + lax.rem(y + i, SUB)
            if i > 0 or dz > 0:
                b_copy(n).start()
            else:
                pltpu.make_async_copy(mid.at[n], xt.at[t], l_sem.at[0]).start()

    for i, dz in enumerate(B_ORDER):
        if i == B_EARLY:
            pl.when(jnp.logical_not(early))(a_start)
        b_steps(dz)
    pltpu.make_async_copy(mid.at[t], xt.at[t], l_sem.at[0]).wait()
    load_band.wait()

    first = lax.rem(lax.rem(z + FREQ - 1, FREQ) // 2, GROUPS)

    def lanes_of(ff):
        return pl.ds(pl.multiple_of(ff * LANES, LANES), LANES)

    def piece(ff, h):
        return pl.ds(pl.multiple_of(ff * PART + H_ROW[h], TILE), H_ROWS[h])

    def c_copy(i, g, h):
        to = freq_peer(i)
        return remote(spec.at[g, piece(to, h), :],
                      held.at[g, pl.ds(H_ROW[h], H_ROWS[h]), lanes_of(f)],
                      c_send.at[g, h], c_recv.at[g, h], (t, to))

    def wait_slab(i):
        n = lax.rem(GROUP * first + i, TM)

        @pl.when(n != t)
        def _():
            remote(xt.at[n], xt.at[n], b_send, b_recv.at[n], (t, f)).wait_recv()

    def make_group(g, h):
        stack = xt[pl.ds(GROUP * g, SLABS)].reshape(DEPTH, LANES)

        def part(i):
            value = jnp.dot(band[piece(freq_peer(i), h), :], stack, preferred_element_type=jnp.float32)
            return value.astype(jnp.bfloat16)

        for i in range(1, FREQ):
            spec[g, piece(freq_peer(i), h), :] = part(i)
            c_copy(i, g, h).start()
        held[g, pl.ds(H_ROW[h], H_ROWS[h]), lanes_of(f)] = part(0)

    def first_half(step):
        lo = jnp.where(step == 0, 0, GROUP * step + 1)
        hi = jnp.minimum(GROUP * step + GROUP + 1, TM)
        each(lo, hi, wait_slab)
        make_group(lax.rem(first + step, GROUPS), 0)

    each(0, GROUPS, first_half)
    each(0, GROUPS, lambda step: make_group(lax.rem(first + step, GROUPS), 1))

    def others(g, h):
        part = held.at[g, pl.ds(H_ROW[h], H_ROWS[h]), pl.ds(0, (FREQ - 1) * LANES)]
        return remote(part, part, c_send.at[g, h], c_recv.at[g, h], (t, f))

    part = mid.at[pl.ds(0, SUB * (FREQ - 1))]
    remote(part, part, a_send, b_send, (t, f)).wait_send()
    part = mid.at[pl.ds(0, TM - 1)]
    remote(part, part, b_send, a_send, (t, f)).wait_send()

    def owner(k):
        return 2 * lax.rem(SPREAD * k, BINS) + f % 2

    def bin_columns(k):
        return jnp.concatenate(
            [held[g, pl.ds(TILE * k, TILE), :] for g in range(GROUPS)], axis=0)

    def g_copy(k):
        return remote(gpart.at[k], grecv.at[t], g_send, g_recv, (owner(k), f))

    def g_start(k):
        @pl.when(owner(k) != t)
        def _():
            g_copy(k).start()

        @pl.when(owner(k) == t)
        def _():
            pltpu.make_async_copy(gpart.at[k], grecv.at[t], l_sem.at[0]).start()

    r = lax.broadcasted_iota(jnp.int32, (64, 64), 0)
    c = lax.broadcasted_iota(jnp.int32, (64, 64), 1)
    block = GROUP * (c // TILE) + c % GROUP
    to_row = BLOCKS * (c % TILE // GROUP) + block
    order = jnp.where((r == to_row) & (block < BLOCKS), 1.0, 0.0).astype(jnp.bfloat16)

    for h in range(2):
        bins = range(H_BIN[h], H_BIN[h + 1])
        each(0, GROUPS, lambda g: others(g, h).wait_recv())
        for k in bins:
            a = bin_columns(k)
            gm = nt_dot(a, a)
            gpart[k] = jnp.concatenate([gm[:32], gm[32:]], axis=1)
        each(bins.start, bins.stop, g_start)
        for k in bins:
            cols[k] = jnp.dot(order, bin_columns(k), preferred_element_type=jnp.float32).astype(
                jnp.bfloat16)

    in_column = t % 2 == f % 2

    def column_bin(zz):
        return lax.rem(SPREAD * ((SUB * zz + y) // 2), BINS)

    def column_has(zz):
        return (SUB * zz + y) // 2 < BINS

    mine = column_bin(z)
    is_owner = in_column & column_has(z)

    def z_copy(i):
        to = SUB * lax.rem(z + i, FREQ) + y
        return remote(res.at[mine], res.at[mine], z_send, z_recv.at[z], (to, f))

    def y_copy(zz, i):
        k = column_bin(zz)
        to = SUB * z + lax.rem(y + i, SUB)
        return remote(res.at[k], res.at[k], y_send, y_recv, (to, f))

    def sized(n, send, recv):
        return remote(grecv.at[pl.ds(0, n)], grecv.at[pl.ds(0, n)], send, recv, (t, f))

    def sends_over(n):
        for h in range(2):
            each(0, GROUPS, lambda g: others(g, h).wait_send())
        sized(n, g_send, y_send).wait_send()

    @pl.when(jnp.logical_not(is_owner))
    def _():
        sends_over(BINS)

    @pl.when(is_owner)
    def _():
        pltpu.make_async_copy(gpart.at[mine], grecv.at[t], l_sem.at[0]).wait()

        sized(TM - 1, y_send, g_recv).wait_recv()
        total = grecv[0]
        for n in range(1, TM):
            total = total + grecv[n]
        total = total * (1.0 / TOTAL_ROWS)
        gm = jnp.concatenate([total[:, :64], total[:, 64:]], axis=0)
        perm[...] = jnp.zeros_like(perm)
        natural_rows(perm, gm)
        gm = perm[0:64, :].T
        natural_rows(perm, gm)
        eye = jnp.where(r == c, 1.0, 0.0).astype(jnp.float32)
        m = jnp.concatenate([perm[0:64, :], eye], axis=1)
        m = eliminate([m[8 * i : 8 * i + 8, :] for i in range(8)])
        m = jnp.concatenate(m, axis=0)
        both = jnp.where(c >= r, m[:, :64], m[:, 64:])
        res[mine] = jnp.concatenate([both[:32], both[32:]], axis=1)
        each(1, FREQ, lambda i: z_copy(i).start())

    def relay(h):
        def step(i):
            zz = lax.rem(z + i, FREQ)
            k = column_bin(zz)

            @pl.when(column_has(zz) & (k >= H_BIN[h]) & (k < H_BIN[h + 1]))
            def _():
                @pl.when(i > 0)
                def _():
                    remote(res.at[k], res.at[k], z_send, z_recv.at[zz], (t, f)).wait_recv()

                for j in range(1, SUB):
                    y_copy(zz, j).start()

        each(0, FREQ, step)

    @pl.when(in_column)
    def _():
        relay(0)
        relay(1)

    @pl.when(is_owner)
    def _():
        sends_over(BINS - 1)
        sized(FREQ - 1, z_send, y_recv).wait_send()

    here = jnp.where(in_column, y // 2, 2)
    held_bins = (FREQ, FREQ - 1)
    for column in range(2):

        @pl.when(here == column)
        def _():
            sized(held_bins[1 - column], z_send, y_recv).wait_recv()
            sized((SUB - 1) * held_bins[column], y_send, y_recv).wait_send()

    @pl.when(here == 2)
    def _():
        sized(BINS, z_send, y_recv).wait_recv()


def last_kernel(cols_hbm, res_hbm, basis_hbm, factor_hbm, cols, res, basis, factor, in_sem, out_sem):
    def chunk(i):
        return pl.ds(LAST_BINS * i, LAST_BINS)

    loads = [pltpu.make_async_copy(res_hbm, res, in_sem.at[CHUNKS])]
    loads += [
        pltpu.make_async_copy(cols_hbm.at[chunk(i)], cols.at[chunk(i)], in_sem.at[i])
        for i in range(CHUNKS)
    ]
    stores = [
        pltpu.make_async_copy(basis.at[chunk(i)], basis_hbm.at[chunk(i)], out_sem.at[i])
        for i in range(CHUNKS)
    ]
    stores.append(pltpu.make_async_copy(factor, factor_hbm, out_sem.at[CHUNKS]))
    for load in loads:
        load.start()
    r = lax.broadcasted_iota(jnp.int32, (64, 64), 0)
    c = lax.broadcasted_iota(jnp.int32, (64, 64), 1)
    loads[0].wait()
    wide = []
    for k in range(BINS):
        v = res[k]
        both = jnp.concatenate([v[:, :64], v[:, 64:]], axis=0)
        factor[k] = jnp.where(c >= r, both, 0.0)[:COLS, :COLS]
        wide.append(jnp.where(c < r, both, jnp.where(c == r, 1.0 / both, 0.0)))
    stores[-1].start()
    for i in range(CHUNKS):
        loads[1 + i].wait()
        for k in range(LAST_BINS * i, LAST_BINS * (i + 1)):
            w = wide[k]
            hi = w.astype(jnp.bfloat16)
            rest = w - hi.astype(jnp.float32)
            lo = rest.astype(jnp.bfloat16)
            low = (rest - lo.astype(jnp.float32)).astype(jnp.bfloat16)
            a = cols[k]
            out = jnp.dot(low, a, preferred_element_type=jnp.float32)
            out = out + jnp.dot(lo, a, preferred_element_type=jnp.float32)
            out = out + jnp.dot(hi, a, preferred_element_type=jnp.float32)
            basis[k] = out[:COLS, :].astype(jnp.bfloat16)
        stores[i].start()
    for store in stores:
        store.wait()


def on_device(snapshots):
    band = jnp.asarray(band_table())
    bf16, f32 = jnp.bfloat16, jnp.float32
    dma = pltpu.SemaphoreType.DMA
    hbm = pl.BlockSpec(memory_space=pltpu.HBM)
    vmem = pl.BlockSpec(memory_space=pltpu.VMEM)
    cols, res = pl.pallas_call(
        kernel,
        out_shape=(
            jax.ShapeDtypeStruct((BINS, 64, ROWS_HERE), bf16),
            jax.ShapeDtypeStruct((BINS, 32, 128), f32),
        ),
        in_specs=[hbm, hbm],
        out_specs=(vmem, vmem),
        scratch_shapes=[
            pltpu.VMEM((K * TILE, DEPTH), bf16),
            pltpu.VMEM((TM, HALF, LANES), bf16),
            pltpu.VMEM((TM + 1, HALF, LANES), bf16),
            pltpu.VMEM((GROUPS, K * TILE, LANES), bf16),
            pltpu.VMEM((GROUPS, PART, ROWS_HERE), bf16),
            pltpu.VMEM((BINS, 32, 128), f32),
            pltpu.VMEM((TM, 32, 128), f32),
            pltpu.VMEM((72, 64), f32),
            dma,
            dma((GROUPS,)),
            dma,
            dma((FREQ,)),
            dma,
            dma((TM,)),
            dma((GROUPS, 2)),
            dma((GROUPS, 2)),
            dma,
            dma,
            dma,
            dma((FREQ,)),
            dma,
            dma,
        ],
        name="block_spectra_qr",
        compiler_params=pltpu.CompilerParams(
            collective_id=0, has_side_effects=True, vmem_limit_bytes=60 * 2**20
        ),
    )(snapshots, band)

    return pl.pallas_call(
        last_kernel,
        out_shape=(
            jax.ShapeDtypeStruct((BINS, COLS, ROWS_HERE), bf16),
            jax.ShapeDtypeStruct((BINS, COLS, COLS), f32),
        ),
        in_specs=[hbm, hbm],
        out_specs=(hbm, hbm),
        scratch_shapes=[
            pltpu.VMEM((BINS, 64, ROWS_HERE), bf16),
            pltpu.VMEM((BINS, 32, 128), f32),
            pltpu.VMEM((BINS, COLS, ROWS_HERE), bf16),
            pltpu.VMEM((BINS, COLS, COLS), f32),
            dma((CHUNKS + 1,)),
            dma((CHUNKS + 1,)),
        ],
        name="basis",
        compiler_params=pltpu.CompilerParams(vmem_limit_bytes=60 * 2**20),
    )(cols, res)


def solution(mesh):
    return jax.shard_map(
        on_device,
        mesh=mesh,
        in_specs=(P("tm", "freq"),),
        out_specs=(P("freq", None, "tm"), P("freq", None, None)),
        check_vma=False,
    )
```

```python
import math

import jax
import jax.numpy as jnp
import numpy as np
from jax import lax
from jax.experimental import pallas as pl
from jax.experimental.pallas import tpu as pltpu
from jax.sharding import PartitionSpec as P

MESH = pl.DeviceIdType.MESH
K = 120
HALF = 128
TM = 32
FREQ = 8
BINS = K // FREQ
BLOCKS = TM - 1
COLS = 2 * BLOCKS
GROUP = 8
GROUPS = TM // GROUP
TILE = 2 * GROUP
PART = BINS * TILE
LANES = 128
SLABS = GROUP + 1
DEPTH = SLABS * HALF
SUB = 4
ROWS_HERE = FREQ * LANES
LAST_BINS = 3
CHUNKS = BINS // LAST_BINS
SPREAD = 11
H_BIN = (0, 11, BINS)
H_ROW = tuple(TILE * k for k in H_BIN[:2])
H_ROWS = tuple(TILE * (hi - lo) for lo, hi in zip(H_BIN, H_BIN[1:]))
B_ORDER = (2, 6, 4, 0, 1, 7, 3, 5)
B_EARLY = 4
TOTAL_ROWS = TM * ROWS_HERE


def band_table():
    bins = np.arange(1, K + 1, dtype=np.int64)[:, None]
    sample = np.arange(2 * HALF, dtype=np.int64)[None, :]
    phase = (bins * sample % (2 * HALF)) * (2.0 * math.pi / (2 * HALF))
    window = 0.5 - 0.5 * np.cos(sample * (2.0 * math.pi / (2 * HALF)))
    table = np.stack([window * np.cos(phase), -window * np.sin(phase)], axis=1)
    table = table.astype(np.float32)
    band = np.zeros((K, 2, GROUP, SLABS * HALF), np.float32)
    for b in range(GROUP):
        band[:, :, b, b * HALF : (b + 2) * HALF] = table
    return band.reshape(K * TILE, DEPTH).astype(jnp.bfloat16)


def nt_dot(a, b):
    return lax.dot_general(a, b, (((1,), (1,)), ((), ())), preferred_element_type=jnp.float32)


def natural_rows(dst, value):
    for p in range(2):
        for g in range(GROUPS):
            r = TILE * g + GROUP * p
            dst[pl.ds(BLOCKS * p + GROUP * g, GROUP), :] = value[r : r + GROUP, :]


def eliminate(m):
    row = lax.broadcasted_iota(jnp.int32, (8, 128), 0)

    def spread(v):
        return jnp.broadcast_to(v, (8, 128))

    for b in range(8):
        j = 8 * b
        width = min(8, COLS - j)
        low = [[spread(m[b][q : q + 1, j + p : j + p + 1]) for p in range(q + 1)] for q in range(width)]
        inv, done = [], []
        for q in range(width):
            for p in range(q):
                low[q][q] = low[q][q] - low[q][p] * low[q][p]
            inv.append(lax.rsqrt(low[q][q]))
            for u in range(q + 1, width):
                for p in range(q):
                    low[u][q] = low[u][q] - low[u][p] * low[q][p]
                low[u][q] = low[u][q] * inv[q]
            v = spread(m[b][q : q + 1, :])
            for p in range(q):
                v = v - low[q][p] * done[p]
            done.append(v * inv[q])
        for i in range(b + 1, 8):
            below = []
            for q in range(width):
                v = spread(m[i][:, j + q : j + q + 1])
                for p in range(q):
                    v = v - low[q][p] * below[p]
                below.append(v * inv[q])
            for q in range(width):
                m[i] = m[i] - below[q] * done[q]
        for q in range(width):
            m[b] = jnp.where(row == q, done[q], m[b])
    return m


def kernel(
    x_ref, band_hbm, cols_hbm, res,
    band, mid, xt, spec, held, cols, gpart, grecv, perm,
    cols_sem, band_sem, l_sem, a_send, a_recv, b_send, b_recv, c_send, c_recv,
    g_send, g_recv, z_send, z_recv, y_send, y_recv,
):
    t = lax.axis_index("tm")
    f = lax.axis_index("freq")
    z, y = t // SUB, t % SUB

    def colblock(j):
        return x_ref.at[:, pl.ds(pl.multiple_of(j * LANES, LANES), LANES)]

    def freq_peer(i):
        return lax.rem(f + i, FREQ)

    def tm_peer(i):
        return lax.rem(t + i, TM)

    def remote(src, dst, send, recv, to):
        return pltpu.make_async_remote_copy(
            src, dst, send, recv, device_id=to, device_id_type=MESH
        )

    def each(lo, hi, body):
        def step(i, carry):
            body(i)
            return carry

        lax.fori_loop(lo, hi, step, 0)

    load_band = pltpu.make_async_copy(band_hbm, band, band_sem)
    load_band.start()

    barrier = pltpu.get_barrier_semaphore()
    each(1, FREQ, lambda i: pl.semaphore_signal(
        barrier, inc=1, device_id=(t, freq_peer(i)), device_id_type=MESH))
    each(1, TM, lambda i: pl.semaphore_signal(
        barrier, inc=1, device_id=(tm_peer(i), f), device_id_type=MESH))
    pl.semaphore_wait(barrier, FREQ - 1 + TM - 1)

    def a_copy(i, s):
        to = freq_peer(i)
        return remote(colblock(FREQ * s + to), mid.at[SUB * f + s], a_send, a_recv.at[f], (t, to))

    def own_copy(s):
        return pltpu.make_async_copy(colblock(FREQ * s + f), mid.at[SUB * f + s], l_sem.at[s])

    away = lax.rem(f - z + FREQ, FREQ)
    early = away % 2 == 0

    def a_start():
        def a_peer(i):
            for s in range(SUB):
                a_copy(i, s).start()

        each(1, FREQ, a_peer)

    pl.when(early)(a_start)
    for s in range(SUB):
        own_copy(s).start()
    xt[TM] = jnp.zeros((HALF, LANES), jnp.bfloat16)
    for s in range(SUB):
        own_copy(s).wait()

    def b_copy(n):
        return remote(mid.at[n], xt.at[t], b_send, b_recv.at[t], (n, f))

    def b_steps(dz):
        ff = lax.rem(z + dz, FREQ)

        @pl.when(ff != f)
        def _():
            part = mid.at[pl.ds(SUB * ff, SUB)]
            remote(part, part, a_send, a_recv.at[ff], (t, f)).wait_recv()

        for i in range(SUB):
            n = SUB * ff + lax.rem(y + i, SUB)
            if i > 0 or dz > 0:
                b_copy(n).start()
            else:
                pltpu.make_async_copy(mid.at[n], xt.at[t], l_sem.at[0]).start()

    for i, dz in enumerate(B_ORDER):
        if i == B_EARLY:
            pl.when(jnp.logical_not(early))(a_start)
        b_steps(dz)
    pltpu.make_async_copy(mid.at[t], xt.at[t], l_sem.at[0]).wait()
    load_band.wait()

    first = lax.rem(lax.rem(z + FREQ - 1, FREQ) // 2, GROUPS)

    def lanes_of(ff):
        return pl.ds(pl.multiple_of(ff * LANES, LANES), LANES)

    def piece(ff, h):
        return pl.ds(pl.multiple_of(ff * PART + H_ROW[h], TILE), H_ROWS[h])

    def c_copy(i, g, h):
        to = freq_peer(i)
        return remote(spec.at[g, piece(to, h), :],
                      held.at[g, pl.ds(H_ROW[h], H_ROWS[h]), lanes_of(f)],
                      c_send.at[g, h], c_recv.at[g, h], (t, to))

    def wait_slab(i):
        n = lax.rem(GROUP * first + i, TM)

        @pl.when(n != t)
        def _():
            remote(xt.at[n], xt.at[n], b_send, b_recv.at[n], (t, f)).wait_recv()

    def make_group(g, h):
        stack = xt[pl.ds(GROUP * g, SLABS)].reshape(DEPTH, LANES)

        def part(i):
            value = jnp.dot(band[piece(freq_peer(i), h), :], stack, preferred_element_type=jnp.float32)
            return value.astype(jnp.bfloat16)

        for i in range(1, FREQ):
            spec[g, piece(freq_peer(i), h), :] = part(i)
            c_copy(i, g, h).start()
        held[g, pl.ds(H_ROW[h], H_ROWS[h]), lanes_of(f)] = part(0)

    def first_half(step):
        lo = jnp.where(step == 0, 0, GROUP * step + 1)
        hi = jnp.minimum(GROUP * step + GROUP + 1, TM)
        each(lo, hi, wait_slab)
        make_group(lax.rem(first + step, GROUPS), 0)

    each(0, GROUPS, first_half)
    each(0, GROUPS, lambda step: make_group(lax.rem(first + step, GROUPS), 1))

    def others(g, h):
        part = held.at[g, pl.ds(H_ROW[h], H_ROWS[h]), pl.ds(0, (FREQ - 1) * LANES)]
        return remote(part, part, c_send.at[g, h], c_recv.at[g, h], (t, f))

    part = mid.at[pl.ds(0, SUB * (FREQ - 1))]
    remote(part, part, a_send, b_send, (t, f)).wait_send()
    part = mid.at[pl.ds(0, TM - 1)]
    remote(part, part, b_send, a_send, (t, f)).wait_send()

    def owner(k):
        return 2 * lax.rem(SPREAD * k, BINS) + f % 2

    def bin_columns(k):
        return jnp.concatenate(
            [held[g, pl.ds(TILE * k, TILE), :] for g in range(GROUPS)], axis=0)

    def g_copy(k):
        return remote(gpart.at[k], grecv.at[t], g_send, g_recv, (owner(k), f))

    def g_start(k):
        @pl.when(owner(k) != t)
        def _():
            g_copy(k).start()

        @pl.when(owner(k) == t)
        def _():
            pltpu.make_async_copy(gpart.at[k], grecv.at[t], l_sem.at[0]).start()

    r = lax.broadcasted_iota(jnp.int32, (64, 64), 0)
    c = lax.broadcasted_iota(jnp.int32, (64, 64), 1)
    block = GROUP * (c // TILE) + c % GROUP
    to_row = BLOCKS * (c % TILE // GROUP) + block
    order = jnp.where((r == to_row) & (block < BLOCKS), 1.0, 0.0).astype(jnp.bfloat16)

    def cols_out(h):
        part = pl.ds(H_BIN[h], H_BIN[h + 1] - H_BIN[h])
        return pltpu.make_async_copy(cols.at[part], cols_hbm.at[part], cols_sem.at[h])

    for h in range(2):
        bins = range(H_BIN[h], H_BIN[h + 1])
        each(0, GROUPS, lambda g: others(g, h).wait_recv())
        for k in bins:
            a = bin_columns(k)
            gm = nt_dot(a, a)
            gpart[k] = jnp.concatenate([gm[:32], gm[32:]], axis=1)
        each(bins.start, bins.stop, g_start)
        for k in bins:
            cols[k] = jnp.dot(order, bin_columns(k), preferred_element_type=jnp.float32).astype(
                jnp.bfloat16)
        cols_out(h).start()

    in_column = t % 2 == f % 2

    def column_bin(zz):
        return lax.rem(SPREAD * ((SUB * zz + y) // 2), BINS)

    def column_has(zz):
        return (SUB * zz + y) // 2 < BINS

    mine = column_bin(z)
    is_owner = in_column & column_has(z)

    def z_copy(i):
        to = SUB * lax.rem(z + i, FREQ) + y
        return remote(res.at[mine], res.at[mine], z_send, z_recv.at[z], (to, f))

    def y_copy(zz, i):
        k = column_bin(zz)
        to = SUB * z + lax.rem(y + i, SUB)
        return remote(res.at[k], res.at[k], y_send, y_recv, (to, f))

    def sized(n, send, recv):
        return remote(grecv.at[pl.ds(0, n)], grecv.at[pl.ds(0, n)], send, recv, (t, f))

    def sends_over(n):
        for h in range(2):
            each(0, GROUPS, lambda g: others(g, h).wait_send())
        sized(n, g_send, y_send).wait_send()

    @pl.when(jnp.logical_not(is_owner))
    def _():
        sends_over(BINS)

    @pl.when(is_owner)
    def _():
        pltpu.make_async_copy(gpart.at[mine], grecv.at[t], l_sem.at[0]).wait()

        sized(TM - 1, y_send, g_recv).wait_recv()
        total = grecv[0]
        for n in range(1, TM):
            total = total + grecv[n]
        total = total * (1.0 / TOTAL_ROWS)
        gm = jnp.concatenate([total[:, :64], total[:, 64:]], axis=0)
        perm[...] = jnp.zeros_like(perm)
        natural_rows(perm, gm)
        gm = perm[0:64, :].T
        natural_rows(perm, gm)
        eye = jnp.where(r == c, 1.0, 0.0).astype(jnp.float32)
        m = jnp.concatenate([perm[0:64, :], eye], axis=1)
        m = eliminate([m[8 * i : 8 * i + 8, :] for i in range(8)])
        m = jnp.concatenate(m, axis=0)
        both = jnp.where(c >= r, m[:, :64], m[:, 64:])
        res[mine] = jnp.concatenate([both[:32], both[32:]], axis=1)
        each(1, FREQ, lambda i: z_copy(i).start())

    def relay(h):
        def step(i):
            zz = lax.rem(z + i, FREQ)
            k = column_bin(zz)

            @pl.when(column_has(zz) & (k >= H_BIN[h]) & (k < H_BIN[h + 1]))
            def _():
                @pl.when(i > 0)
                def _():
                    remote(res.at[k], res.at[k], z_send, z_recv.at[zz], (t, f)).wait_recv()

                for j in range(1, SUB):
                    y_copy(zz, j).start()

        each(0, FREQ, step)

    @pl.when(in_column)
    def _():
        relay(0)
        relay(1)

    @pl.when(is_owner)
    def _():
        sends_over(BINS - 1)
        sized(FREQ - 1, z_send, y_recv).wait_send()

    for h in range(2):
        cols_out(h).wait()

    here = jnp.where(in_column, y // 2, 2)
    held_bins = (FREQ, FREQ - 1)
    for column in range(2):

        @pl.when(here == column)
        def _():
            sized(held_bins[1 - column], z_send, y_recv).wait_recv()
            sized((SUB - 1) * held_bins[column], y_send, y_recv).wait_send()

    @pl.when(here == 2)
    def _():
        sized(BINS, z_send, y_recv).wait_recv()


def last_kernel(cols_hbm, res_hbm, basis_hbm, factor_hbm, cols, res, basis, factor, in_sem, out_sem):
    def chunk(i):
        return pl.ds(LAST_BINS * i, LAST_BINS)

    loads = [pltpu.make_async_copy(res_hbm, res, in_sem.at[CHUNKS])]
    loads += [
        pltpu.make_async_copy(cols_hbm.at[chunk(i)], cols.at[chunk(i)], in_sem.at[i])
        for i in range(CHUNKS)
    ]
    stores = [
        pltpu.make_async_copy(basis.at[chunk(i)], basis_hbm.at[chunk(i)], out_sem.at[i])
        for i in range(CHUNKS)
    ]
    stores.append(pltpu.make_async_copy(factor, factor_hbm, out_sem.at[CHUNKS]))
    for load in loads:
        load.start()
    r = lax.broadcasted_iota(jnp.int32, (64, 64), 0)
    c = lax.broadcasted_iota(jnp.int32, (64, 64), 1)
    loads[0].wait()
    wide = []
    for k in range(BINS):
        v = res[k]
        both = jnp.concatenate([v[:, :64], v[:, 64:]], axis=0)
        factor[k] = jnp.where(c >= r, both, 0.0)[:COLS, :COLS]
        wide.append(jnp.where(c < r, both, jnp.where(c == r, 1.0 / both, 0.0)))
    stores[-1].start()
    for i in range(CHUNKS):
        loads[1 + i].wait()
        for k in range(LAST_BINS * i, LAST_BINS * (i + 1)):
            w = wide[k]
            hi = w.astype(jnp.bfloat16)
            rest = w - hi.astype(jnp.float32)
            lo = rest.astype(jnp.bfloat16)
            low = (rest - lo.astype(jnp.float32)).astype(jnp.bfloat16)
            a = cols[k]
            out = jnp.dot(low, a, preferred_element_type=jnp.float32)
            out = out + jnp.dot(lo, a, preferred_element_type=jnp.float32)
            out = out + jnp.dot(hi, a, preferred_element_type=jnp.float32)
            basis[k] = out[:COLS, :].astype(jnp.bfloat16)
        stores[i].start()
    for store in stores:
        store.wait()


def on_device(snapshots):
    band = jnp.asarray(band_table())
    bf16, f32 = jnp.bfloat16, jnp.float32
    dma = pltpu.SemaphoreType.DMA
    hbm = pl.BlockSpec(memory_space=pltpu.HBM)
    vmem = pl.BlockSpec(memory_space=pltpu.VMEM)
    cols, res = pl.pallas_call(
        kernel,
        out_shape=(
            jax.ShapeDtypeStruct((BINS, 64, ROWS_HERE), bf16),
            jax.ShapeDtypeStruct((BINS, 32, 128), f32),
        ),
        in_specs=[hbm, hbm],
        out_specs=(hbm, vmem),
        scratch_shapes=[
            pltpu.VMEM((K * TILE, DEPTH), bf16),
            pltpu.VMEM((TM, HALF, LANES), bf16),
            pltpu.VMEM((TM + 1, HALF, LANES), bf16),
            pltpu.VMEM((GROUPS, K * TILE, LANES), bf16),
            pltpu.VMEM((GROUPS, PART, ROWS_HERE), bf16),
            pltpu.VMEM((BINS, 64, ROWS_HERE), bf16),
            pltpu.VMEM((BINS, 32, 128), f32),
            pltpu.VMEM((TM, 32, 128), f32),
            pltpu.VMEM((72, 64), f32),
            dma((2,)),
            dma,
            dma((GROUPS,)),
            dma,
            dma((FREQ,)),
            dma,
            dma((TM,)),
            dma((GROUPS, 2)),
            dma((GROUPS, 2)),
            dma,
            dma,
            dma,
            dma((FREQ,)),
            dma,
            dma,
        ],
        name="block_spectra_qr",
        compiler_params=pltpu.CompilerParams(
            collective_id=0, has_side_effects=True, vmem_limit_bytes=60 * 2**20
        ),
    )(snapshots, band)

    return pl.pallas_call(
        last_kernel,
        out_shape=(
            jax.ShapeDtypeStruct((BINS, COLS, ROWS_HERE), bf16),
            jax.ShapeDtypeStruct((BINS, COLS, COLS), f32),
        ),
        in_specs=[hbm, hbm],
        out_specs=(hbm, hbm),
        scratch_shapes=[
            pltpu.VMEM((BINS, 64, ROWS_HERE), bf16),
            pltpu.VMEM((BINS, 32, 128), f32),
            pltpu.VMEM((BINS, COLS, ROWS_HERE), bf16),
            pltpu.VMEM((BINS, COLS, COLS), f32),
            dma((CHUNKS + 1,)),
            dma((CHUNKS + 1,)),
        ],
        name="basis",
        compiler_params=pltpu.CompilerParams(vmem_limit_bytes=60 * 2**20),
    )(cols, res)


def solution(mesh):
    return jax.shard_map(
        on_device,
        mesh=mesh,
        in_specs=(P("tm", "freq"),),
        out_specs=(P("freq", None, "tm"), P("freq", None, None)),
        check_vma=False,
    )
```

```python
import math

import jax
import jax.numpy as jnp
import numpy as np
from jax import lax
from jax.experimental import pallas as pl
from jax.experimental.pallas import tpu as pltpu
from jax.sharding import PartitionSpec as P

MESH = pl.DeviceIdType.MESH
K = 120
HALF = 128
TM = 32
FREQ = 8
BINS = K // FREQ
BLOCKS = TM - 1
COLS = 2 * BLOCKS
GROUP = 8
GROUPS = TM // GROUP
TILE = 2 * GROUP
PART = BINS * TILE
LANES = 128
SLABS = GROUP + 1
DEPTH = SLABS * HALF
SUB = 4
ROWS_HERE = FREQ * LANES
LAST_BINS = 3
CHUNKS = BINS // LAST_BINS
SPREAD = 11
H_BIN = (0, 11, BINS)
H_ROW = tuple(TILE * k for k in H_BIN[:2])
H_ROWS = tuple(TILE * (hi - lo) for lo, hi in zip(H_BIN, H_BIN[1:]))
Z_ORDER = (4, 3, 5, 2, 6, 1, 7)
X_ORDER = (2, 6, 4, 3, 7, 5, 1)
B_EARLY = ((2, 6, 4), (0,))
B_LATE = ((1, 7), (3, 5))
TOTAL_ROWS = TM * ROWS_HERE


def band_table():
    bins = np.arange(1, K + 1, dtype=np.int64)[:, None]
    sample = np.arange(2 * HALF, dtype=np.int64)[None, :]
    phase = (bins * sample % (2 * HALF)) * (2.0 * math.pi / (2 * HALF))
    window = 0.5 - 0.5 * np.cos(sample * (2.0 * math.pi / (2 * HALF)))
    table = np.stack([window * np.cos(phase), -window * np.sin(phase)], axis=1)
    table = table.astype(np.float32)
    band = np.zeros((K, 2, GROUP, SLABS * HALF), np.float32)
    for b in range(GROUP):
        band[:, :, b, b * HALF : (b + 2) * HALF] = table
    return band.reshape(K * TILE, DEPTH).astype(jnp.bfloat16)


def nt_dot(a, b):
    return lax.dot_general(a, b, (((1,), (1,)), ((), ())), preferred_element_type=jnp.float32)


def natural_rows(dst, value):
    for p in range(2):
        for g in range(GROUPS):
            r = TILE * g + GROUP * p
            dst[pl.ds(BLOCKS * p + GROUP * g, GROUP), :] = value[r : r + GROUP, :]


def eliminate(m):
    row = lax.broadcasted_iota(jnp.int32, (8, 128), 0)

    def spread(v):
        return jnp.broadcast_to(v, (8, 128))

    for b in range(8):
        j = 8 * b
        width = min(8, COLS - j)
        low = [[spread(m[b][q : q + 1, j + p : j + p + 1]) for p in range(q + 1)] for q in range(width)]
        inv, done = [], []
        for q in range(width):
            for p in range(q):
                low[q][q] = low[q][q] - low[q][p] * low[q][p]
            inv.append(lax.rsqrt(low[q][q]))
            for u in range(q + 1, width):
                for p in range(q):
                    low[u][q] = low[u][q] - low[u][p] * low[q][p]
                low[u][q] = low[u][q] * inv[q]
            v = spread(m[b][q : q + 1, :])
            for p in range(q):
                v = v - low[q][p] * done[p]
            done.append(v * inv[q])
        for i in range(b + 1, 8):
            below = []
            for q in range(width):
                v = spread(m[i][:, j + q : j + q + 1])
                for p in range(q):
                    v = v - low[q][p] * below[p]
                below.append(v * inv[q])
            for q in range(width):
                m[i] = m[i] - below[q] * done[q]
        for q in range(width):
            m[b] = jnp.where(row == q, done[q], m[b])
    return m


def kernel(
    x_ref, band_hbm, cols_hbm, res,
    band, mid, xt, spec, held, cols, gpart, grecv, perm,
    cols_sem, band_sem, l_sem, a_send, a_recv, b_send, b_recv, c_send, c_recv,
    g_send, g_recv, z_send, z_recv, y_send, y_recv,
):
    t = lax.axis_index("tm")
    f = lax.axis_index("freq")
    z, y = t // SUB, t % SUB

    def colblock(j):
        return x_ref.at[:, pl.ds(pl.multiple_of(j * LANES, LANES), LANES)]

    def freq_peer(i):
        return lax.rem(f + i, FREQ)

    def tm_peer(i):
        return lax.rem(t + i, TM)

    def remote(src, dst, send, recv, to):
        return pltpu.make_async_remote_copy(
            src, dst, send, recv, device_id=to, device_id_type=MESH
        )

    def each(lo, hi, body):
        def step(i, carry):
            body(i)
            return carry

        lax.fori_loop(lo, hi, step, 0)

    load_band = pltpu.make_async_copy(band_hbm, band, band_sem)
    load_band.start()

    barrier = pltpu.get_barrier_semaphore()
    for i in range(1, FREQ):
        pl.semaphore_signal(barrier, inc=1, device_id=(t, freq_peer(i)), device_id_type=MESH)
    for i in range(1, TM):
        pl.semaphore_signal(barrier, inc=1, device_id=(tm_peer(i), f), device_id_type=MESH)
    pl.semaphore_wait(barrier, FREQ - 1 + TM - 1)

    def a_copy(i, s):
        to = freq_peer(i)
        return remote(colblock(FREQ * s + to), mid.at[SUB * f + s], a_send, a_recv.at[f], (t, to))

    def own_copy(s):
        return pltpu.make_async_copy(colblock(FREQ * s + f), mid.at[SUB * f + s], l_sem.at[s])

    away = lax.rem(f - z + FREQ, FREQ)
    early = away % 2 == 0

    def a_start():
        def a_peer(i):
            for s in range(SUB):
                a_copy(i, s).start()

        for i in X_ORDER:
            a_peer(i)

    pl.when(early)(a_start)
    for s in range(SUB):
        own_copy(s).start()
    xt[TM] = jnp.zeros((HALF, LANES), jnp.bfloat16)
    for s in range(SUB):
        own_copy(s).wait()

    def b_copy(n):
        return remote(mid.at[n], xt.at[t], b_send, b_recv.at[t], (n, f))

    def b_round(planes):
        sources = [(dz, lax.rem(z + dz, FREQ)) for dz in planes]
        for _, ff in sources:

            @pl.when(ff != f)
            def _():
                part = mid.at[pl.ds(SUB * ff, SUB)]
                remote(part, part, a_send, a_recv.at[ff], (t, f)).wait_recv()

        for i in range(SUB):
            for dz, ff in sources:
                n = SUB * ff + lax.rem(y + i, SUB)
                if i > 0 or dz > 0:
                    b_copy(n).start()
                else:
                    pltpu.make_async_copy(mid.at[n], xt.at[t], l_sem.at[0]).start()

    for planes in B_EARLY:
        b_round(planes)
    pl.when(jnp.logical_not(early))(a_start)
    for planes in B_LATE:
        b_round(planes)
    pltpu.make_async_copy(mid.at[t], xt.at[t], l_sem.at[0]).wait()
    load_band.wait()

    first = lax.rem(lax.rem(z + FREQ - 1, FREQ) // 2, GROUPS)

    def lanes_of(ff):
        return pl.ds(pl.multiple_of(ff * LANES, LANES), LANES)

    def piece(ff, h):
        return pl.ds(pl.multiple_of(ff * PART + H_ROW[h], TILE), H_ROWS[h])

    def c_copy(i, g, h):
        to = freq_peer(i)
        return remote(spec.at[g, piece(to, h), :],
                      held.at[g, pl.ds(H_ROW[h], H_ROWS[h]), lanes_of(f)],
                      c_send.at[g, h], c_recv.at[g, h], (t, to))

    def wait_slab(i):
        n = lax.rem(GROUP * first + i, TM)

        @pl.when(n != t)
        def _():
            remote(xt.at[n], xt.at[n], b_send, b_recv.at[n], (t, f)).wait_recv()

    def make_group(g, h):
        stack = xt[pl.ds(GROUP * g, SLABS)].reshape(DEPTH, LANES)

        def part(i):
            value = jnp.dot(band[piece(freq_peer(i), h), :], stack, preferred_element_type=jnp.float32)
            return value.astype(jnp.bfloat16)

        for i in X_ORDER:
            spec[g, piece(freq_peer(i), h), :] = part(i)
            c_copy(i, g, h).start()
        held[g, pl.ds(H_ROW[h], H_ROWS[h]), lanes_of(f)] = part(0)

    def first_half(step):
        lo = jnp.where(step == 0, 0, GROUP * step + 1)
        hi = jnp.minimum(GROUP * step + GROUP + 1, TM)
        each(lo, hi, wait_slab)
        make_group(lax.rem(first + step, GROUPS), 0)

    each(0, GROUPS, first_half)
    each(0, GROUPS, lambda step: make_group(lax.rem(first + step, GROUPS), 1))

    def others(g, h):
        part = held.at[g, pl.ds(H_ROW[h], H_ROWS[h]), pl.ds(0, (FREQ - 1) * LANES)]
        return remote(part, part, c_send.at[g, h], c_recv.at[g, h], (t, f))

    part = mid.at[pl.ds(0, SUB * (FREQ - 1))]
    remote(part, part, a_send, b_send, (t, f)).wait_send()
    part = mid.at[pl.ds(0, TM - 1)]
    remote(part, part, b_send, a_send, (t, f)).wait_send()

    def owner(k):
        return 2 * lax.rem(SPREAD * k, BINS) + f % 2

    def bin_columns(k):
        return jnp.concatenate(
            [held[g, pl.ds(TILE * k, TILE), :] for g in range(GROUPS)], axis=0)

    def g_copy(k):
        return remote(gpart.at[k], grecv.at[t], g_send, g_recv, (owner(k), f))

    def g_start(k):
        @pl.when(owner(k) != t)
        def _():
            g_copy(k).start()

        @pl.when(owner(k) == t)
        def _():
            pltpu.make_async_copy(gpart.at[k], grecv.at[t], l_sem.at[0]).start()

    r = lax.broadcasted_iota(jnp.int32, (64, 64), 0)
    c = lax.broadcasted_iota(jnp.int32, (64, 64), 1)
    block = GROUP * (c // TILE) + c % GROUP
    to_row = BLOCKS * (c % TILE // GROUP) + block
    order = jnp.where((r == to_row) & (block < BLOCKS), 1.0, 0.0).astype(jnp.bfloat16)

    def cols_out(h):
        part = pl.ds(H_BIN[h], H_BIN[h + 1] - H_BIN[h])
        return pltpu.make_async_copy(cols.at[part], cols_hbm.at[part], cols_sem.at[h])

    for h in range(2):
        bins = range(H_BIN[h], H_BIN[h + 1])
        each(0, GROUPS, lambda g: others(g, h).wait_recv())
        for k in bins:
            a = bin_columns(k)
            gm = nt_dot(a, a)
            gpart[k] = jnp.concatenate([gm[:32], gm[32:]], axis=1)
        for i in range(len(bins)):
            g_start(bins.start + lax.rem(t + i, len(bins)))
        for k in bins:
            cols[k] = jnp.dot(order, bin_columns(k), preferred_element_type=jnp.float32).astype(
                jnp.bfloat16)
        cols_out(h).start()

    in_column = t % 2 == f % 2

    def column_bin(zz):
        return lax.rem(SPREAD * ((SUB * zz + y) // 2), BINS)

    def column_has(zz):
        return (SUB * zz + y) // 2 < BINS

    mine = column_bin(z)
    is_owner = in_column & column_has(z)

    def z_copy(i):
        to = SUB * lax.rem(z + i, FREQ) + y
        return remote(res.at[mine], res.at[mine], z_send, z_recv.at[z], (to, f))

    def y_copy(zz, i):
        k = column_bin(zz)
        to = SUB * z + lax.rem(y + i, SUB)
        return remote(res.at[k], res.at[k], y_send, y_recv, (to, f))

    def sized(n, send, recv):
        return remote(grecv.at[pl.ds(0, n)], grecv.at[pl.ds(0, n)], send, recv, (t, f))

    def sends_over(n):
        for h in range(2):
            each(0, GROUPS, lambda g: others(g, h).wait_send())
        sized(n, g_send, y_send).wait_send()

    @pl.when(jnp.logical_not(is_owner))
    def _():
        sends_over(BINS)

    @pl.when(is_owner)
    def _():
        pltpu.make_async_copy(gpart.at[mine], grecv.at[t], l_sem.at[0]).wait()

        sized(TM - 1, y_send, g_recv).wait_recv()
        total = grecv[0]
        for n in range(1, TM):
            total = total + grecv[n]
        total = total * (1.0 / TOTAL_ROWS)
        gm = jnp.concatenate([total[:, :64], total[:, 64:]], axis=0)
        perm[...] = jnp.zeros_like(perm)
        natural_rows(perm, gm)
        gm = perm[0:64, :].T
        natural_rows(perm, gm)
        eye = jnp.where(r == c, 1.0, 0.0).astype(jnp.float32)
        m = jnp.concatenate([perm[0:64, :], eye], axis=1)
        m = eliminate([m[8 * i : 8 * i + 8, :] for i in range(8)])
        m = jnp.concatenate(m, axis=0)
        both = jnp.where(c >= r, m[:, :64], m[:, 64:])
        res[mine] = jnp.concatenate([both[:32], both[32:]], axis=1)
        for i in Z_ORDER:
            z_copy(i).start()

    def relay(h):
        def step(i):
            zz = lax.rem(z + i, FREQ)
            k = column_bin(zz)

            @pl.when(column_has(zz) & (k >= H_BIN[h]) & (k < H_BIN[h + 1]))
            def _():
                if i > 0:
                    remote(res.at[k], res.at[k], z_send, z_recv.at[zz], (t, f)).wait_recv()

                for j in range(1, SUB):
                    y_copy(zz, j).start()

        for i in (0, *reversed(Z_ORDER)):
            step(i)

    @pl.when(in_column)
    def _():
        relay(0)
        relay(1)

    @pl.when(is_owner)
    def _():
        sends_over(BINS - 1)
        sized(FREQ - 1, z_send, y_recv).wait_send()

    for h in range(2):
        cols_out(h).wait()

    here = jnp.where(in_column, y // 2, 2)
    held_bins = (FREQ, FREQ - 1)
    for column in range(2):

        @pl.when(here == column)
        def _():
            sized(held_bins[1 - column], z_send, y_recv).wait_recv()
            sized((SUB - 1) * held_bins[column], y_send, y_recv).wait_send()

    @pl.when(here == 2)
    def _():
        sized(BINS, z_send, y_recv).wait_recv()


def last_kernel(cols_hbm, res_hbm, basis_hbm, factor_hbm, cols, res, basis, factor, in_sem, out_sem):
    def chunk(i):
        return pl.ds(LAST_BINS * i, LAST_BINS)

    loads = [pltpu.make_async_copy(res_hbm, res, in_sem.at[CHUNKS])]
    loads += [
        pltpu.make_async_copy(cols_hbm.at[chunk(i)], cols.at[chunk(i)], in_sem.at[i])
        for i in range(CHUNKS)
    ]
    stores = [
        pltpu.make_async_copy(basis.at[chunk(i)], basis_hbm.at[chunk(i)], out_sem.at[i])
        for i in range(CHUNKS)
    ]
    stores.append(pltpu.make_async_copy(factor, factor_hbm, out_sem.at[CHUNKS]))
    for load in loads:
        load.start()
    r = lax.broadcasted_iota(jnp.int32, (64, 64), 0)
    c = lax.broadcasted_iota(jnp.int32, (64, 64), 1)
    loads[0].wait()
    wide = []
    for k in range(BINS):
        v = res[k]
        both = jnp.concatenate([v[:, :64], v[:, 64:]], axis=0)
        factor[k] = jnp.where(c >= r, both, 0.0)[:COLS, :COLS]
        wide.append(jnp.where(c < r, both, jnp.where(c == r, 1.0 / both, 0.0)))
    stores[-1].start()
    for i in range(CHUNKS):
        loads[1 + i].wait()
        for k in range(LAST_BINS * i, LAST_BINS * (i + 1)):
            w = wide[k]
            hi = w.astype(jnp.bfloat16)
            rest = w - hi.astype(jnp.float32)
            lo = rest.astype(jnp.bfloat16)
            low = (rest - lo.astype(jnp.float32)).astype(jnp.bfloat16)
            a = cols[k]
            out = jnp.dot(low, a, preferred_element_type=jnp.float32)
            out = out + jnp.dot(lo, a, preferred_element_type=jnp.float32)
            out = out + jnp.dot(hi, a, preferred_element_type=jnp.float32)
            basis[k] = out[:COLS, :].astype(jnp.bfloat16)
        stores[i].start()
    for store in stores:
        store.wait()


def on_device(snapshots):
    band = jnp.asarray(band_table())
    bf16, f32 = jnp.bfloat16, jnp.float32
    dma = pltpu.SemaphoreType.DMA
    hbm = pl.BlockSpec(memory_space=pltpu.HBM)
    vmem = pl.BlockSpec(memory_space=pltpu.VMEM)
    cols, res = pl.pallas_call(
        kernel,
        out_shape=(
            jax.ShapeDtypeStruct((BINS, 64, ROWS_HERE), bf16),
            jax.ShapeDtypeStruct((BINS, 32, 128), f32),
        ),
        in_specs=[hbm, hbm],
        out_specs=(hbm, vmem),
        scratch_shapes=[
            pltpu.VMEM((K * TILE, DEPTH), bf16),
            pltpu.VMEM((TM, HALF, LANES), bf16),
            pltpu.VMEM((TM + 1, HALF, LANES), bf16),
            pltpu.VMEM((GROUPS, K * TILE, LANES), bf16),
            pltpu.VMEM((GROUPS, PART, ROWS_HERE), bf16),
            pltpu.VMEM((BINS, 64, ROWS_HERE), bf16),
            pltpu.VMEM((BINS, 32, 128), f32),
            pltpu.VMEM((TM, 32, 128), f32),
            pltpu.VMEM((72, 64), f32),
            dma((2,)),
            dma,
            dma((GROUPS,)),
            dma,
            dma((FREQ,)),
            dma,
            dma((TM,)),
            dma((GROUPS, 2)),
            dma((GROUPS, 2)),
            dma,
            dma,
            dma,
            dma((FREQ,)),
            dma,
            dma,
        ],
        name="block_spectra_qr",
        compiler_params=pltpu.CompilerParams(
            collective_id=0, has_side_effects=True, vmem_limit_bytes=60 * 2**20
        ),
    )(snapshots, band)

    return pl.pallas_call(
        last_kernel,
        out_shape=(
            jax.ShapeDtypeStruct((BINS, COLS, ROWS_HERE), bf16),
            jax.ShapeDtypeStruct((BINS, COLS, COLS), f32),
        ),
        in_specs=[hbm, hbm],
        out_specs=(hbm, hbm),
        scratch_shapes=[
            pltpu.VMEM((BINS, 64, ROWS_HERE), bf16),
            pltpu.VMEM((BINS, 32, 128), f32),
            pltpu.VMEM((BINS, COLS, ROWS_HERE), bf16),
            pltpu.VMEM((BINS, COLS, COLS), f32),
            dma((CHUNKS + 1,)),
            dma((CHUNKS + 1,)),
        ],
        name="basis",
        compiler_params=pltpu.CompilerParams(vmem_limit_bytes=60 * 2**20),
    )(cols, res)


def solution(mesh):
    return jax.shard_map(
        on_device,
        mesh=mesh,
        in_specs=(P("tm", "freq"),),
        out_specs=(P("freq", None, "tm"), P("freq", None, None)),
        check_vma=False,
    )
```

```python
import math

import jax
import jax.numpy as jnp
import numpy as np
from jax import lax
from jax.experimental import pallas as pl
from jax.experimental.pallas import tpu as pltpu
from jax.sharding import PartitionSpec as P

MESH = pl.DeviceIdType.MESH
K = 120
HALF = 128
TM = 32
FREQ = 8
BINS = K // FREQ
BLOCKS = TM - 1
COLS = 2 * BLOCKS
GROUP = 8
GROUPS = TM // GROUP
TILE = 2 * GROUP
PART = BINS * TILE
LANES = 128
SLABS = GROUP + 1
DEPTH = SLABS * HALF
SUB = 4
ROWS_HERE = FREQ * LANES
LAST_BINS = 5
SPREAD = 11
H_BIN = (0, 11, BINS)
H_ROW = tuple(TILE * k for k in H_BIN[:2])
H_ROWS = tuple(TILE * (hi - lo) for lo, hi in zip(H_BIN, H_BIN[1:]))
Z_ORDER = (4, 3, 5, 2, 6, 1, 7)
X_ORDER = (2, 6, 4, 3, 7, 5, 1)
B_EARLY = ((2, 6, 4), (0,))
B_LATE = ((1, 7), (3, 5))
TOTAL_ROWS = TM * ROWS_HERE


def band_table():
    bins = np.arange(1, K + 1, dtype=np.int64)[:, None]
    sample = np.arange(2 * HALF, dtype=np.int64)[None, :]
    phase = (bins * sample % (2 * HALF)) * (2.0 * math.pi / (2 * HALF))
    window = 0.5 - 0.5 * np.cos(sample * (2.0 * math.pi / (2 * HALF)))
    table = np.stack([window * np.cos(phase), -window * np.sin(phase)], axis=1)
    table = table.astype(np.float32)
    band = np.zeros((K, 2, GROUP, SLABS * HALF), np.float32)
    for b in range(GROUP):
        band[:, :, b, b * HALF : (b + 2) * HALF] = table
    return band.reshape(K * TILE, DEPTH).astype(jnp.bfloat16)


def nt_dot(a, b):
    return lax.dot_general(a, b, (((1,), (1,)), ((), ())), preferred_element_type=jnp.float32)


def natural_rows(dst, value):
    for p in range(2):
        for g in range(GROUPS):
            r = TILE * g + GROUP * p
            dst[pl.ds(BLOCKS * p + GROUP * g, GROUP), :] = value[r : r + GROUP, :]


def eliminate(m):
    row = lax.broadcasted_iota(jnp.int32, (8, 128), 0)

    def spread(v):
        return jnp.broadcast_to(v, (8, 128))

    for b in range(8):
        j = 8 * b
        width = min(8, COLS - j)
        low = [[spread(m[b][q : q + 1, j + p : j + p + 1]) for p in range(q + 1)] for q in range(width)]
        inv, done = [], []
        for q in range(width):
            for p in range(q):
                low[q][q] = low[q][q] - low[q][p] * low[q][p]
            inv.append(lax.rsqrt(low[q][q]))
            for u in range(q + 1, width):
                for p in range(q):
                    low[u][q] = low[u][q] - low[u][p] * low[q][p]
                low[u][q] = low[u][q] * inv[q]
            v = spread(m[b][q : q + 1, :])
            for p in range(q):
                v = v - low[q][p] * done[p]
            done.append(v * inv[q])
        for i in range(b + 1, 8):
            below = []
            for q in range(width):
                v = spread(m[i][:, j + q : j + q + 1])
                for p in range(q):
                    v = v - low[q][p] * below[p]
                below.append(v * inv[q])
            for q in range(width):
                m[i] = m[i] - below[q] * done[q]
        for q in range(width):
            m[b] = jnp.where(row == q, done[q], m[b])
    return m


def kernel(
    x_ref, band_hbm, cols_hbm, res,
    band, mid, xt, spec, held, cols, gpart, grecv, perm,
    cols_sem, band_sem, l_sem, a_send, a_recv, b_send, b_recv, c_send, c_recv,
    g_send, g_recv, z_send, z_recv, y_send, y_recv,
):
    t = lax.axis_index("tm")
    f = lax.axis_index("freq")
    z, y = t // SUB, t % SUB

    def colblock(j):
        return x_ref.at[:, pl.ds(pl.multiple_of(j * LANES, LANES), LANES)]

    def freq_peer(i):
        return lax.rem(f + i, FREQ)

    def tm_peer(i):
        return lax.rem(t + i, TM)

    def remote(src, dst, send, recv, to):
        return pltpu.make_async_remote_copy(
            src, dst, send, recv, device_id=to, device_id_type=MESH
        )

    def each(lo, hi, body):
        def step(i, carry):
            body(i)
            return carry

        lax.fori_loop(lo, hi, step, 0)

    load_band = pltpu.make_async_copy(band_hbm, band, band_sem)
    load_band.start()

    barrier = pltpu.get_barrier_semaphore()
    for i in range(1, FREQ):
        pl.semaphore_signal(barrier, inc=1, device_id=(t, freq_peer(i)), device_id_type=MESH)
    for i in range(1, TM):
        pl.semaphore_signal(barrier, inc=1, device_id=(tm_peer(i), f), device_id_type=MESH)
    pl.semaphore_wait(barrier, FREQ - 1 + TM - 1)

    def a_copy(i, s):
        to = freq_peer(i)
        return remote(colblock(FREQ * s + to), mid.at[SUB * f + s], a_send, a_recv.at[f], (t, to))

    def own_copy(s):
        return pltpu.make_async_copy(colblock(FREQ * s + f), mid.at[SUB * f + s], l_sem.at[s])

    away = lax.rem(f - z + FREQ, FREQ)
    early = away % 2 == 0

    def a_start():
        def a_peer(i):
            for s in range(SUB):
                a_copy(i, s).start()

        for i in X_ORDER:
            a_peer(i)

    pl.when(early)(a_start)
    for s in range(SUB):
        own_copy(s).start()
    xt[TM] = jnp.zeros((HALF, LANES), jnp.bfloat16)
    for s in range(SUB):
        own_copy(s).wait()

    def b_copy(n):
        return remote(mid.at[n], xt.at[t], b_send, b_recv.at[t], (n, f))

    def b_round(planes):
        sources = [(dz, lax.rem(z + dz, FREQ)) for dz in planes]
        for _, ff in sources:

            @pl.when(ff != f)
            def _():
                part = mid.at[pl.ds(SUB * ff, SUB)]
                remote(part, part, a_send, a_recv.at[ff], (t, f)).wait_recv()

        for i in range(SUB):
            for dz, ff in sources:
                n = SUB * ff + lax.rem(y + i, SUB)
                if i > 0 or dz > 0:
                    b_copy(n).start()
                else:
                    pltpu.make_async_copy(mid.at[n], xt.at[t], l_sem.at[0]).start()

    for planes in B_EARLY:
        b_round(planes)
    pl.when(jnp.logical_not(early))(a_start)
    for planes in B_LATE:
        b_round(planes)
    pltpu.make_async_copy(mid.at[t], xt.at[t], l_sem.at[0]).wait()
    load_band.wait()

    first = lax.rem(lax.rem(z + FREQ - 1, FREQ) // 2, GROUPS)

    def lanes_of(ff):
        return pl.ds(pl.multiple_of(ff * LANES, LANES), LANES)

    def piece(ff, h):
        return pl.ds(pl.multiple_of(ff * PART + H_ROW[h], TILE), H_ROWS[h])

    def c_copy(i, g, h):
        to = freq_peer(i)
        return remote(spec.at[g, piece(to, h), :],
                      held.at[g, pl.ds(H_ROW[h], H_ROWS[h]), lanes_of(f)],
                      c_send.at[g, h], c_recv.at[g, h], (t, to))

    def wait_slab(i):
        n = lax.rem(GROUP * first + i, TM)

        @pl.when(n != t)
        def _():
            remote(xt.at[n], xt.at[n], b_send, b_recv.at[n], (t, f)).wait_recv()

    def make_group(g, h):
        stack = xt[pl.ds(GROUP * g, SLABS)].reshape(DEPTH, LANES)

        def part(i):
            value = jnp.dot(band[piece(freq_peer(i), h), :], stack, preferred_element_type=jnp.float32)
            return value.astype(jnp.bfloat16)

        for i in X_ORDER:
            spec[g, piece(freq_peer(i), h), :] = part(i)
            c_copy(i, g, h).start()
        held[g, pl.ds(H_ROW[h], H_ROWS[h]), lanes_of(f)] = part(0)

    def first_half(step):
        lo = jnp.where(step == 0, 0, GROUP * step + 1)
        hi = jnp.minimum(GROUP * step + GROUP + 1, TM)
        each(lo, hi, wait_slab)
        make_group(lax.rem(first + step, GROUPS), 0)

    each(0, GROUPS, first_half)
    each(0, GROUPS, lambda step: make_group(lax.rem(first + step, GROUPS), 1))

    def others(g, h):
        part = held.at[g, pl.ds(H_ROW[h], H_ROWS[h]), pl.ds(0, (FREQ - 1) * LANES)]
        return remote(part, part, c_send.at[g, h], c_recv.at[g, h], (t, f))

    part = mid.at[pl.ds(0, SUB * (FREQ - 1))]
    remote(part, part, a_send, b_send, (t, f)).wait_send()
    part = mid.at[pl.ds(0, TM - 1)]
    remote(part, part, b_send, a_send, (t, f)).wait_send()

    def owner(k):
        return 2 * lax.rem(SPREAD * k, BINS) + f % 2

    def bin_columns(k):
        return jnp.concatenate(
            [held[g, pl.ds(TILE * k, TILE), :] for g in range(GROUPS)], axis=0)

    def g_copy(k):
        return remote(gpart.at[k], grecv.at[t], g_send, g_recv, (owner(k), f))

    def g_start(k):
        @pl.when(owner(k) != t)
        def _():
            g_copy(k).start()

        @pl.when(owner(k) == t)
        def _():
            pltpu.make_async_copy(gpart.at[k], grecv.at[t], l_sem.at[0]).start()

    r = lax.broadcasted_iota(jnp.int32, (64, 64), 0)
    c = lax.broadcasted_iota(jnp.int32, (64, 64), 1)
    block = GROUP * (c // TILE) + c % GROUP
    to_row = BLOCKS * (c % TILE // GROUP) + block
    order = jnp.where((r == to_row) & (block < BLOCKS), 1.0, 0.0).astype(jnp.bfloat16)

    def cols_out(h):
        part = pl.ds(H_BIN[h], H_BIN[h + 1] - H_BIN[h])
        return pltpu.make_async_copy(cols.at[part], cols_hbm.at[part], cols_sem.at[h])

    for h in range(2):
        bins = range(H_BIN[h], H_BIN[h + 1])
        each(0, GROUPS, lambda g: others(g, h).wait_recv())
        for k in bins:
            a = bin_columns(k)
            gm = nt_dot(a, a)
            gpart[k] = jnp.concatenate([gm[:32], gm[32:]], axis=1)
        for i in range(len(bins)):
            g_start(bins.start + lax.rem(t + i, len(bins)))
        for k in bins:
            cols[k] = jnp.dot(order, bin_columns(k), preferred_element_type=jnp.float32).astype(
                jnp.bfloat16)
        cols_out(h).start()

    in_column = t % 2 == f % 2

    def column_bin(zz):
        return lax.rem(SPREAD * ((SUB * zz + y) // 2), BINS)

    def column_has(zz):
        return (SUB * zz + y) // 2 < BINS

    mine = column_bin(z)
    is_owner = in_column & column_has(z)

    def z_copy(i):
        to = SUB * lax.rem(z + i, FREQ) + y
        return remote(res.at[mine], res.at[mine], z_send, z_recv.at[z], (to, f))

    def y_copy(zz, i):
        k = column_bin(zz)
        to = SUB * z + lax.rem(y + i, SUB)
        return remote(res.at[k], res.at[k], y_send, y_recv, (to, f))

    def sized(n, send, recv):
        return remote(grecv.at[pl.ds(0, n)], grecv.at[pl.ds(0, n)], send, recv, (t, f))

    def sends_over(n):
        for h in range(2):
            each(0, GROUPS, lambda g: others(g, h).wait_send())
        sized(n, g_send, y_send).wait_send()

    @pl.when(jnp.logical_not(is_owner))
    def _():
        sends_over(BINS)

    @pl.when(is_owner)
    def _():
        pltpu.make_async_copy(gpart.at[mine], grecv.at[t], l_sem.at[0]).wait()

        sized(TM - 1, y_send, g_recv).wait_recv()
        total = grecv[0]
        for n in range(1, TM):
            total = total + grecv[n]
        total = total * (1.0 / TOTAL_ROWS)
        gm = jnp.concatenate([total[:, :64], total[:, 64:]], axis=0)
        perm[...] = jnp.zeros_like(perm)
        natural_rows(perm, gm)
        gm = perm[0:64, :].T
        natural_rows(perm, gm)
        eye = jnp.where(r == c, 1.0, 0.0).astype(jnp.float32)
        m = jnp.concatenate([perm[0:64, :], eye], axis=1)
        m = eliminate([m[8 * i : 8 * i + 8, :] for i in range(8)])
        m = jnp.concatenate(m, axis=0)
        both = jnp.where(c >= r, m[:, :64], m[:, 64:])
        res[mine] = jnp.concatenate([both[:32], both[32:]], axis=1)
        for i in Z_ORDER:
            z_copy(i).start()

    def relay(h):
        def step(i):
            zz = lax.rem(z + i, FREQ)
            k = column_bin(zz)

            @pl.when(column_has(zz) & (k >= H_BIN[h]) & (k < H_BIN[h + 1]))
            def _():
                if i > 0:
                    remote(res.at[k], res.at[k], z_send, z_recv.at[zz], (t, f)).wait_recv()

                for j in range(1, SUB):
                    y_copy(zz, j).start()

        for i in (0, *reversed(Z_ORDER)):
            step(i)

    @pl.when(in_column)
    def _():
        relay(0)
        relay(1)

    @pl.when(is_owner)
    def _():
        sends_over(BINS - 1)
        sized(FREQ - 1, z_send, y_recv).wait_send()

    for h in range(2):
        cols_out(h).wait()

    here = jnp.where(in_column, y // 2, 2)
    held_bins = (FREQ, FREQ - 1)
    for column in range(2):

        @pl.when(here == column)
        def _():
            sized(held_bins[1 - column], z_send, y_recv).wait_recv()
            sized((SUB - 1) * held_bins[column], y_send, y_recv).wait_send()

    @pl.when(here == 2)
    def _():
        sized(BINS, z_send, y_recv).wait_recv()


def last_kernel(cols, res, basis, factor):
    r = lax.broadcasted_iota(jnp.int32, (64, 64), 0)
    c = lax.broadcasted_iota(jnp.int32, (64, 64), 1)
    for k in range(LAST_BINS):
        v = res[k]
        both = jnp.concatenate([v[:, :64], v[:, 64:]], axis=0)
        factor[k] = jnp.where(c >= r, both, 0.0)[:COLS, :COLS]
        w = jnp.where(c < r, both, jnp.where(c == r, 1.0 / both, 0.0))
        hi = w.astype(jnp.bfloat16)
        rest = w - hi.astype(jnp.float32)
        lo = rest.astype(jnp.bfloat16)
        low = (rest - lo.astype(jnp.float32)).astype(jnp.bfloat16)
        a = cols[k]
        out = jnp.dot(low, a, preferred_element_type=jnp.float32)
        out = out + jnp.dot(lo, a, preferred_element_type=jnp.float32)
        out = out + jnp.dot(hi, a, preferred_element_type=jnp.float32)
        basis[k] = out[:COLS, :].astype(jnp.bfloat16)


def on_device(snapshots):
    band = jnp.asarray(band_table())
    bf16, f32 = jnp.bfloat16, jnp.float32
    dma = pltpu.SemaphoreType.DMA
    hbm = pl.BlockSpec(memory_space=pltpu.HBM)
    vmem = pl.BlockSpec(memory_space=pltpu.VMEM)
    cols, res = pl.pallas_call(
        kernel,
        out_shape=(
            jax.ShapeDtypeStruct((BINS, 64, ROWS_HERE), bf16),
            jax.ShapeDtypeStruct((BINS, 32, 128), f32),
        ),
        in_specs=[hbm, hbm],
        out_specs=(hbm, vmem),
        scratch_shapes=[
            pltpu.VMEM((K * TILE, DEPTH), bf16),
            pltpu.VMEM((TM, HALF, LANES), bf16),
            pltpu.VMEM((TM + 1, HALF, LANES), bf16),
            pltpu.VMEM((GROUPS, K * TILE, LANES), bf16),
            pltpu.VMEM((GROUPS, PART, ROWS_HERE), bf16),
            pltpu.VMEM((BINS, 64, ROWS_HERE), bf16),
            pltpu.VMEM((BINS, 32, 128), f32),
            pltpu.VMEM((TM, 32, 128), f32),
            pltpu.VMEM((72, 64), f32),
            dma((2,)),
            dma,
            dma((GROUPS,)),
            dma,
            dma((FREQ,)),
            dma,
            dma((TM,)),
            dma((GROUPS, 2)),
            dma((GROUPS, 2)),
            dma,
            dma,
            dma,
            dma((FREQ,)),
            dma,
            dma,
        ],
        name="block_spectra_qr",
        compiler_params=pltpu.CompilerParams(
            collective_id=0, has_side_effects=True, vmem_limit_bytes=60 * 2**20
        ),
    )(snapshots, band)

    def blocks(*shape):
        return pl.BlockSpec((LAST_BINS, *shape), lambda i: (i, 0, 0))

    return pl.pallas_call(
        last_kernel,
        grid=(BINS // LAST_BINS,),
        out_shape=(
            jax.ShapeDtypeStruct((BINS, COLS, ROWS_HERE), bf16),
            jax.ShapeDtypeStruct((BINS, COLS, COLS), f32),
        ),
        in_specs=[blocks(64, ROWS_HERE), blocks(32, 128)],
        out_specs=(blocks(COLS, ROWS_HERE), blocks(COLS, COLS)),
        name="basis",
        compiler_params=pltpu.CompilerParams(vmem_limit_bytes=60 * 2**20),
    )(cols, res)


def solution(mesh):
    return jax.shard_map(
        on_device,
        mesh=mesh,
        in_specs=(P("tm", "freq"),),
        out_specs=(P("freq", None, "tm"), P("freq", None, None)),
        check_vma=False,
    )
```

```python
import math

import jax
import jax.numpy as jnp
import numpy as np
from jax import lax
from jax.experimental import pallas as pl
from jax.experimental.pallas import tpu as pltpu
from jax.sharding import PartitionSpec as P

MESH = pl.DeviceIdType.MESH
K = 120
HALF = 128
TM = 32
FREQ = 8
BINS = K // FREQ
BLOCKS = TM - 1
COLS = 2 * BLOCKS
GROUP = 8
GROUPS = TM // GROUP
TILE = 2 * GROUP
PART = BINS * TILE
LANES = 128
SLABS = GROUP + 1
DEPTH = SLABS * HALF
SUB = 4
ROWS_HERE = FREQ * LANES
LAST_BINS = 5
SPREAD = 11
H_BIN = (0, 12, BINS)
H_ROW = tuple(TILE * k for k in H_BIN[:2])
H_ROWS = tuple(TILE * (hi - lo) for lo, hi in zip(H_BIN, H_BIN[1:]))
Z_ORDER = (4, 3, 5, 2, 6, 1, 7)
X_ORDER = (2, 6, 4, 3, 7, 5, 1)
B_EARLY = ((2, 6, 4), (0,))
B_LATE = ((1, 7), (3, 5))
TOTAL_ROWS = TM * ROWS_HERE


def band_table():
    bins = np.arange(1, K + 1, dtype=np.int64)[:, None]
    sample = np.arange(2 * HALF, dtype=np.int64)[None, :]
    phase = (bins * sample % (2 * HALF)) * (2.0 * math.pi / (2 * HALF))
    window = 0.5 - 0.5 * np.cos(sample * (2.0 * math.pi / (2 * HALF)))
    table = np.stack([window * np.cos(phase), -window * np.sin(phase)], axis=1)
    table = table.astype(np.float32)
    band = np.zeros((K, 2, GROUP, SLABS * HALF), np.float32)
    for b in range(GROUP):
        band[:, :, b, b * HALF : (b + 2) * HALF] = table
    return band.reshape(K * TILE, DEPTH).astype(jnp.bfloat16)


def nt_dot(a, b):
    return lax.dot_general(a, b, (((1,), (1,)), ((), ())), preferred_element_type=jnp.float32)


def natural_rows(dst, value):
    for p in range(2):
        for g in range(GROUPS):
            r = TILE * g + GROUP * p
            dst[pl.ds(BLOCKS * p + GROUP * g, GROUP), :] = value[r : r + GROUP, :]


def eliminate(m):
    row = lax.broadcasted_iota(jnp.int32, (8, 128), 0)

    def spread(v):
        return jnp.broadcast_to(v, (8, 128))

    for b in range(8):
        j = 8 * b
        width = min(8, COLS - j)
        low = [[spread(m[b][q : q + 1, j + p : j + p + 1]) for p in range(q + 1)] for q in range(width)]
        inv, done = [], []
        for q in range(width):
            for p in range(q):
                low[q][q] = low[q][q] - low[q][p] * low[q][p]
            inv.append(lax.rsqrt(low[q][q]))
            for u in range(q + 1, width):
                for p in range(q):
                    low[u][q] = low[u][q] - low[u][p] * low[q][p]
                low[u][q] = low[u][q] * inv[q]
            v = spread(m[b][q : q + 1, :])
            for p in range(q):
                v = v - low[q][p] * done[p]
            done.append(v * inv[q])
        for i in range(b + 1, 8):
            below = []
            for q in range(width):
                v = spread(m[i][:, j + q : j + q + 1])
                for p in range(q):
                    v = v - low[q][p] * below[p]
                below.append(v * inv[q])
            for q in range(width):
                m[i] = m[i] - below[q] * done[q]
        for q in range(width):
            m[b] = jnp.where(row == q, done[q], m[b])
    return m


def kernel(
    x_ref, band_hbm, cols_hbm, res,
    band, mid, xt, spec, held, cols, gpart, grecv, perm,
    cols_sem, band_sem, l_sem, a_send, a_recv, b_send, b_recv, c_send, c_recv,
    g_send, g_recv, z_send, z_recv, y_send, y_recv,
):
    t = lax.axis_index("tm")
    f = lax.axis_index("freq")
    z, y = t // SUB, t % SUB

    def colblock(j):
        return x_ref.at[:, pl.ds(pl.multiple_of(j * LANES, LANES), LANES)]

    def freq_peer(i):
        return lax.rem(f + i, FREQ)

    def tm_peer(i):
        return lax.rem(t + i, TM)

    def remote(src, dst, send, recv, to):
        return pltpu.make_async_remote_copy(
            src, dst, send, recv, device_id=to, device_id_type=MESH
        )

    def each(lo, hi, body):
        def step(i, carry):
            body(i)
            return carry

        lax.fori_loop(lo, hi, step, 0)

    load_band = pltpu.make_async_copy(band_hbm, band, band_sem)
    load_band.start()

    barrier = pltpu.get_barrier_semaphore()
    for i in range(1, FREQ):
        pl.semaphore_signal(barrier, inc=1, device_id=(t, freq_peer(i)), device_id_type=MESH)
    for i in range(1, TM):
        pl.semaphore_signal(barrier, inc=1, device_id=(tm_peer(i), f), device_id_type=MESH)
    pl.semaphore_wait(barrier, FREQ - 1 + TM - 1)

    def a_copy(i, s):
        to = freq_peer(i)
        return remote(colblock(FREQ * s + to), mid.at[SUB * f + s], a_send, a_recv.at[f], (t, to))

    def own_copy(s):
        return pltpu.make_async_copy(colblock(FREQ * s + f), mid.at[SUB * f + s], l_sem.at[s])

    away = lax.rem(f - z + FREQ, FREQ)
    early = away % 2 == 0

    def a_start():
        def a_peer(i):
            for s in range(SUB):
                a_copy(i, s).start()

        for i in X_ORDER:
            a_peer(i)

    pl.when(early)(a_start)
    for s in range(SUB):
        own_copy(s).start()
    xt[TM] = jnp.zeros((HALF, LANES), jnp.bfloat16)
    for s in range(SUB):
        own_copy(s).wait()

    def b_copy(n):
        return remote(mid.at[n], xt.at[t], b_send, b_recv.at[t], (n, f))

    def b_round(planes):
        sources = [(dz, lax.rem(z + dz, FREQ)) for dz in planes]
        for _, ff in sources:

            @pl.when(ff != f)
            def _():
                part = mid.at[pl.ds(SUB * ff, SUB)]
                remote(part, part, a_send, a_recv.at[ff], (t, f)).wait_recv()

        for i in range(SUB):
            for dz, ff in sources:
                n = SUB * ff + lax.rem(y + i, SUB)
                if i > 0 or dz > 0:
                    b_copy(n).start()
                else:
                    pltpu.make_async_copy(mid.at[n], xt.at[t], l_sem.at[0]).start()

    for planes in B_EARLY:
        b_round(planes)
    pl.when(jnp.logical_not(early))(a_start)
    for planes in B_LATE:
        b_round(planes)
    pltpu.make_async_copy(mid.at[t], xt.at[t], l_sem.at[0]).wait()
    load_band.wait()

    first = lax.rem(lax.rem(z + FREQ - 1, FREQ) // 2, GROUPS)

    def lanes_of(ff):
        return pl.ds(pl.multiple_of(ff * LANES, LANES), LANES)

    def piece(ff, h):
        return pl.ds(pl.multiple_of(ff * PART + H_ROW[h], TILE), H_ROWS[h])

    def c_copy(i, g, h):
        to = freq_peer(i)
        return remote(spec.at[g, piece(to, h), :],
                      held.at[g, pl.ds(H_ROW[h], H_ROWS[h]), lanes_of(f)],
                      c_send.at[g, h], c_recv.at[g, h], (t, to))

    def wait_slab(i):
        n = lax.rem(GROUP * first + i, TM)

        @pl.when(n != t)
        def _():
            remote(xt.at[n], xt.at[n], b_send, b_recv.at[n], (t, f)).wait_recv()

    def make_group(g, h):
        stack = xt[pl.ds(GROUP * g, SLABS)].reshape(DEPTH, LANES)

        def part(i):
            value = jnp.dot(band[piece(freq_peer(i), h), :], stack, preferred_element_type=jnp.float32)
            return value.astype(jnp.bfloat16)

        for i in X_ORDER:
            spec[g, piece(freq_peer(i), h), :] = part(i)
            c_copy(i, g, h).start()
        held[g, pl.ds(H_ROW[h], H_ROWS[h]), lanes_of(f)] = part(0)

    def first_half(step):
        lo = jnp.where(step == 0, 0, GROUP * step + 1)
        hi = jnp.minimum(GROUP * step + GROUP + 1, TM)
        each(lo, hi, wait_slab)
        make_group(lax.rem(first + step, GROUPS), 0)

    each(0, GROUPS, first_half)
    each(0, GROUPS, lambda step: make_group(lax.rem(first + step, GROUPS), 1))

    def others(g, h):
        part = held.at[g, pl.ds(H_ROW[h], H_ROWS[h]), pl.ds(0, (FREQ - 1) * LANES)]
        return remote(part, part, c_send.at[g, h], c_recv.at[g, h], (t, f))

    part = mid.at[pl.ds(0, SUB * (FREQ - 1))]
    remote(part, part, a_send, b_send, (t, f)).wait_send()
    part = mid.at[pl.ds(0, TM - 1)]
    remote(part, part, b_send, a_send, (t, f)).wait_send()

    def owner(k):
        return 2 * lax.rem(SPREAD * k, BINS) + f % 2

    def bin_columns(k):
        return jnp.concatenate(
            [held[g, pl.ds(TILE * k, TILE), :] for g in range(GROUPS)], axis=0)

    def g_copy(k):
        return remote(gpart.at[k], grecv.at[t], g_send, g_recv, (owner(k), f))

    def g_start(k):
        @pl.when(owner(k) != t)
        def _():
            g_copy(k).start()

        @pl.when(owner(k) == t)
        def _():
            pltpu.make_async_copy(gpart.at[k], grecv.at[t], l_sem.at[0]).start()

    r = lax.broadcasted_iota(jnp.int32, (64, 64), 0)
    c = lax.broadcasted_iota(jnp.int32, (64, 64), 1)
    block = GROUP * (c // TILE) + c % GROUP
    to_row = BLOCKS * (c % TILE // GROUP) + block
    order = jnp.where((r == to_row) & (block < BLOCKS), 1.0, 0.0).astype(jnp.bfloat16)

    def cols_out(h):
        part = pl.ds(H_BIN[h], H_BIN[h + 1] - H_BIN[h])
        return pltpu.make_async_copy(cols.at[part], cols_hbm.at[part], cols_sem.at[h])

    for h in range(2):
        bins = range(H_BIN[h], H_BIN[h + 1])
        each(0, GROUPS, lambda g: others(g, h).wait_recv())
        for k in bins:
            a = bin_columns(k)
            gm = nt_dot(a, a)
            gpart[k] = jnp.concatenate([gm[:32], gm[32:]], axis=1)
        for i in range(len(bins)):
            g_start(bins.start + lax.rem(t + i, len(bins)))
        for k in bins:
            cols[k] = jnp.dot(order, bin_columns(k), preferred_element_type=jnp.float32).astype(
                jnp.bfloat16)
        cols_out(h).start()

    in_column = t % 2 == f % 2

    def column_bin(zz):
        return lax.rem(SPREAD * ((SUB * zz + y) // 2), BINS)

    def column_has(zz):
        return (SUB * zz + y) // 2 < BINS

    mine = column_bin(z)
    is_owner = in_column & column_has(z)

    def z_copy(i):
        to = SUB * lax.rem(z + i, FREQ) + y
        return remote(res.at[mine], res.at[mine], z_send, z_recv.at[z], (to, f))

    def y_copy(zz, i):
        k = column_bin(zz)
        to = SUB * z + lax.rem(y + i, SUB)
        return remote(res.at[k], res.at[k], y_send, y_recv, (to, f))

    def sized(n, send, recv):
        return remote(grecv.at[pl.ds(0, n)], grecv.at[pl.ds(0, n)], send, recv, (t, f))

    def sends_over(n):
        for h in range(2):
            each(0, GROUPS, lambda g: others(g, h).wait_send())
        sized(n, g_send, y_send).wait_send()

    @pl.when(jnp.logical_not(is_owner))
    def _():
        sends_over(BINS)

    @pl.when(is_owner)
    def _():
        pltpu.make_async_copy(gpart.at[mine], grecv.at[t], l_sem.at[0]).wait()

        sized(TM - 1, y_send, g_recv).wait_recv()
        total = grecv[0]
        for n in range(1, TM):
            total = total + grecv[n]
        total = total * (1.0 / TOTAL_ROWS)
        gm = jnp.concatenate([total[:, :64], total[:, 64:]], axis=0)
        perm[...] = jnp.zeros_like(perm)
        natural_rows(perm, gm)
        gm = perm[0:64, :].T
        natural_rows(perm, gm)
        eye = jnp.where(r == c, 1.0, 0.0).astype(jnp.float32)
        m = jnp.concatenate([perm[0:64, :], eye], axis=1)
        m = eliminate([m[8 * i : 8 * i + 8, :] for i in range(8)])
        m = jnp.concatenate(m, axis=0)
        both = jnp.where(c >= r, m[:, :64], m[:, 64:])
        res[mine] = jnp.concatenate([both[:32], both[32:]], axis=1)
        for i in Z_ORDER:
            z_copy(i).start()

    def relay(h):
        def step(i):
            zz = lax.rem(z + i, FREQ)
            k = column_bin(zz)

            @pl.when(column_has(zz) & (k >= H_BIN[h]) & (k < H_BIN[h + 1]))
            def _():
                if i > 0:
                    remote(res.at[k], res.at[k], z_send, z_recv.at[zz], (t, f)).wait_recv()

                for j in (2, 1, 3):
                    y_copy(zz, j).start()

        for i in (0, *reversed(Z_ORDER)):
            step(i)

    @pl.when(in_column)
    def _():
        relay(0)
        relay(1)

    @pl.when(is_owner)
    def _():
        sends_over(BINS - 1)
        sized(FREQ - 1, z_send, y_recv).wait_send()

    for h in range(2):
        cols_out(h).wait()

    here = jnp.where(in_column, y // 2, 2)
    held_bins = (FREQ, FREQ - 1)
    for column in range(2):

        @pl.when(here == column)
        def _():
            sized(held_bins[1 - column], z_send, y_recv).wait_recv()
            sized((SUB - 1) * held_bins[column], y_send, y_recv).wait_send()

    @pl.when(here == 2)
    def _():
        sized(BINS, z_send, y_recv).wait_recv()


def last_kernel(cols, res, basis, factor):
    r = lax.broadcasted_iota(jnp.int32, (64, 64), 0)
    c = lax.broadcasted_iota(jnp.int32, (64, 64), 1)
    for k in range(LAST_BINS):
        v = res[k]
        both = jnp.concatenate([v[:, :64], v[:, 64:]], axis=0)
        factor[k] = jnp.where(c >= r, both, 0.0)[:COLS, :COLS]
        w = jnp.where(c < r, both, jnp.where(c == r, 1.0 / both, 0.0))
        hi = w.astype(jnp.bfloat16)
        rest = w - hi.astype(jnp.float32)
        lo = rest.astype(jnp.bfloat16)
        low = (rest - lo.astype(jnp.float32)).astype(jnp.bfloat16)
        a = cols[k]
        out = jnp.dot(low, a, preferred_element_type=jnp.float32)
        out = out + jnp.dot(lo, a, preferred_element_type=jnp.float32)
        out = out + jnp.dot(hi, a, preferred_element_type=jnp.float32)
        basis[k] = out[:COLS, :].astype(jnp.bfloat16)


def on_device(snapshots):
    band = jnp.asarray(band_table())
    bf16, f32 = jnp.bfloat16, jnp.float32
    dma = pltpu.SemaphoreType.DMA
    hbm = pl.BlockSpec(memory_space=pltpu.HBM)
    vmem = pl.BlockSpec(memory_space=pltpu.VMEM)
    cols, res = pl.pallas_call(
        kernel,
        out_shape=(
            jax.ShapeDtypeStruct((BINS, 64, ROWS_HERE), bf16),
            jax.ShapeDtypeStruct((BINS, 32, 128), f32),
        ),
        in_specs=[hbm, hbm],
        out_specs=(hbm, vmem),
        scratch_shapes=[
            pltpu.VMEM((K * TILE, DEPTH), bf16),
            pltpu.VMEM((TM, HALF, LANES), bf16),
            pltpu.VMEM((TM + 1, HALF, LANES), bf16),
            pltpu.VMEM((GROUPS, K * TILE, LANES), bf16),
            pltpu.VMEM((GROUPS, PART, ROWS_HERE), bf16),
            pltpu.VMEM((BINS, 64, ROWS_HERE), bf16),
            pltpu.VMEM((BINS, 32, 128), f32),
            pltpu.VMEM((TM, 32, 128), f32),
            pltpu.VMEM((72, 64), f32),
            dma((2,)),
            dma,
            dma((GROUPS,)),
            dma,
            dma((FREQ,)),
            dma,
            dma((TM,)),
            dma((GROUPS, 2)),
            dma((GROUPS, 2)),
            dma,
            dma,
            dma,
            dma((FREQ,)),
            dma,
            dma,
        ],
        name="block_spectra_qr",
        compiler_params=pltpu.CompilerParams(
            collective_id=0, has_side_effects=True, vmem_limit_bytes=60 * 2**20
        ),
    )(snapshots, band)

    def blocks(*shape):
        return pl.BlockSpec((LAST_BINS, *shape), lambda i: (i, 0, 0))

    return pl.pallas_call(
        last_kernel,
        grid=(BINS // LAST_BINS,),
        out_shape=(
            jax.ShapeDtypeStruct((BINS, COLS, ROWS_HERE), bf16),
            jax.ShapeDtypeStruct((BINS, COLS, COLS), f32),
        ),
        in_specs=[blocks(64, ROWS_HERE), blocks(32, 128)],
        out_specs=(blocks(COLS, ROWS_HERE), blocks(COLS, COLS)),
        name="basis",
        compiler_params=pltpu.CompilerParams(vmem_limit_bytes=60 * 2**20),
    )(cols, res)


def solution(mesh):
    return jax.shard_map(
        on_device,
        mesh=mesh,
        in_specs=(P("tm", "freq"),),
        out_specs=(P("freq", None, "tm"), P("freq", None, None)),
        check_vma=False,
    )
```
